256 devices in a mesh: owner: 64 (over x, z, core), dense: 4 (over y).
Axes of the slice: x: 4, y: 4, z: 8, core: 2. Of those that a mesh axis runs over, the one named last changes fastest.
Arguments:
- owners: int32 [65536, 13, 4], P(('owner', 'dense')), may hold values from 0 to 63, all different within a row; in each aligned block of 3328 rows (0 to 3327, 3328 to 6655, ..., all dimensions but the last counted through in order) at most 416 rows name the same one
- local_rows: int32 [65536, 13, 4], P(('owner', 'dense')), may hold values from 0 to 2047, as said below
- weights: float32 [65536, 13, 4], P(('owner', 'dense')), may hold values from 0.25 to 4
- labels: bfloat16 [65536], P(('owner', 'dense')), may hold values from 0 to 1
- table: float32 [131072, 128], P('owner'), may hold values from -6 to 6
- accum: float32 [131072], P('owner'), may hold values from 0.0001 to 0.01
- w_in: bfloat16 [1664, 4096], P(None, 'dense'), may hold values from -0.15625 to 0.15625
- b_in: bfloat16 [4096], P('dense'), may hold values from -3 to 3
- w_out: bfloat16 [4096], P('dense'), may hold values from -0.29882812 to 0.29882812
Outputs:
- new_table: float32 [131072, 128], P('owner')
- new_accum: float32 [131072], P('owner')
- weight_grad: float32 [65536, 13, 4], P(('owner', 'dense'))
The draws below stay inside these ranges and needn't reach their ends.
Inputs may be any that keep to these rules, and one draw needn't show every extreme that they name: The 4 owners of one bag differ. Among the bags of one device (3328 of them, aligned blocks of rows), at most 416 name one owner. Among the ids of one device's samples (13312 of them, aligned blocks of rows), exactly 104 distinct values of local_rows occur.
All inputs are finite; a program needn't handle non-finite values.
Results may differ from the reference program's by a relative error of at most 0.0056.
Values may be sent and summed in bfloat16 or wider, within the bound.
No kernel may reach another device: no remote copies, remote signals or barrier semaphores. Data moves between devices by JAX's collectives and lax.ppermute only.
A program may use at most 128 MiB of HBM per device.

```python
import math
import jax
import jax.numpy as jnp
import numpy as np
from jax import lax

E = 128
F = 13
L = 4
H = 4096
S_DEV = 256
ROWS_DEV = 2048
CAP = 416
UNIQ = 104
SAMPLES = 65536
ROWS = 131072
N_OWNER = 64


def draw_local_rows(key, part):
    device_count = SAMPLES // S_DEV
    per_device = S_DEV * F * L

    def one_device(dev_key):
        pool_key, first_key, second_key = jax.random.split(dev_key, 3)
        pool = jax.random.permutation(pool_key, ROWS_DEV)[:UNIQ]
        first_pick = jax.random.randint(first_key, (per_device,), 0, UNIQ)
        second_pick = jax.random.randint(second_key, (per_device,), 0, UNIQ)
        picked = jnp.minimum(first_pick, second_pick)
        picked = picked.at[:UNIQ].set(jnp.arange(UNIQ, dtype=picked.dtype))
        return pool[picked]
    dev_keys = jax.random.split(jax.random.fold_in(key, 71), device_count)
    return jax.vmap(one_device)(dev_keys).reshape(SAMPLES, F, L).astype(jnp.int32)


def shard_levels(own_key, shape, cuts, smallest, high):
    factor_of = 1.0
    for axis_at, shards_of in cuts:
        heights = jax.random.uniform(jax.random.fold_in(jax.random.fold_in(own_key, 6), axis_at), (shards_of,), jnp.float32, smallest / len(cuts), high / len(cuts))
        factor_of = factor_of * jnp.repeat(jnp.exp(heights), shape[axis_at] // shards_of).reshape((-1,) + (1,) * (len(shape) - 1 - axis_at))
    return factor_of


def deal_out(own_key, own, number, rows, amount, top, bound, lean):
    order = jax.random.permutation(own_key, amount)
    heavy_load, usual = load_shares(amount, rows * top, bound, lean, True), load_shares(amount, rows * top, bound, lean, False)
    places = jnp.arange(amount)

    def named(tallies, offset_by):
        used = int((tallies > 0).sum())
        fixed = max(1, used // 4)
        shifted = fixed + (places - fixed + offset_by * (used - fixed)) % max(1, amount - fixed)
        return jnp.zeros((amount,), jnp.int32).at[order[jnp.where(places < fixed, places, shifted)]].set(jnp.asarray(tallies, jnp.int32))

    tallies = jnp.where(number % 4 == 0, named(heavy_load, number // 4), named(usual, number - number // 4 - 1))
    mixed = jax.random.permutation(jax.random.fold_in(own, 3), amount)
    source_of, taker = mixed[0:amount // 2 * 2:2], mixed[1:amount // 2 * 2:2]
    slack = jnp.minimum(tallies[source_of] - 1, bound - tallies[taker]) // 2
    slack = jnp.where((source_of == order[0]) | (taker == order[0]) | (tallies[taker] == 0), 0, jnp.maximum(slack, 0))
    shifted = jax.random.randint(jax.random.fold_in(own, 4), (amount // 2,), 0, 1 << 20) % (slack + 1)
    tallies = tallies.at[source_of].add(-shifted).at[taker].add(shifted)
    items = jnp.searchsorted(jnp.cumsum(tallies), jnp.arange(rows * top), side="right").astype(jnp.int32)
    grid = items.reshape(top, rows).T
    grid = grid[jax.random.permutation(jax.random.fold_in(own, 1), rows)]
    offset_by = jax.random.randint(jax.random.fold_in(own, 2), (rows, 1), 0, top)
    return jnp.take_along_axis(grid, (jnp.arange(top)[None, :] + offset_by) % top, axis=1)


def load_shares(amount, total, reach, lean, full):
    portions = [(1 << 20) // math.isqrt(rank ** lean) + 1 for rank in range(1, amount + 1)]
    largest = reach if full else min(reach, max(-(-total // amount), total * portions[0] // sum(portions)))
    least = 1 if total - largest >= amount - 1 else 0
    holding, spare = [largest] + [least] * (amount - 1), total - largest - least * (amount - 1)
    while spare > 0:
        free = [i for i in range(1, amount) if holding[i] < largest] or [i for i in range(1, amount) if holding[i] < reach]
        whole, budget = sum([portions[i] for i in free]), spare
        for i in free:
            addition = min(reach - holding[i], max(1, budget * portions[i] // whole), spare)
            holding[i] = holding[i] + addition
            spare = spare - addition
    return np.array(holding)


def centred(stream_key, shape, width, bound, cuts=(), kind=jnp.bfloat16):
    gain = shard_levels(stream_key, shape, cuts, -0.22, 0.18) if cuts else 1.0
    values = jax.random.normal(stream_key, shape, jnp.float32) * width * gain
    return jnp.minimum(jnp.maximum(values, -bound), bound).astype(kind)


def setup_inputs(seed: int = 0) -> dict:
    seeds = jax.random.split(jax.random.key(seed), 10)
    owners_keys = jax.random.split(jax.random.fold_in(seeds[0], 1), SAMPLES * F // (S_DEV * F))
    owners_turns = jax.random.permutation(jax.random.fold_in(seeds[0], 3), SAMPLES * F // (S_DEV * F))
    owners = jax.vmap(lambda own, number: deal_out(jax.random.fold_in(seeds[0], 2), own, number, S_DEV * F, N_OWNER, L, CAP, 2))(owners_keys, owners_turns).reshape((SAMPLES, F, L))
    local_rows = draw_local_rows(jax.random.fold_in(seeds[9], 71), 0)
    weights = jnp.clip(jnp.exp(math.log(4.0) - 2.7725887 * jax.random.uniform(seeds[2], (SAMPLES, F, L), jnp.float32) ** shard_levels(seeds[2], (SAMPLES, F, L), ((0, 256),), -0.2, 0.2)), 0.25, 4.0)
    labels = jnp.clip(1.0 * jax.random.uniform(seeds[3], (SAMPLES,), jnp.float32) ** shard_levels(seeds[3], (SAMPLES,), ((0, 256),), -0.2, 0.2), 0.0, 1.0).astype(jnp.bfloat16)
    table = centred(seeds[4], (ROWS, E), 1.0, 6.0, ((0, 64),), jnp.float32)
    accum = jnp.clip(jnp.exp(math.log(0.01) - 4.6051702 * jax.random.uniform(seeds[5], (ROWS,), jnp.float32) ** shard_levels(seeds[5], (ROWS,), ((0, 64),), -0.2, 0.2)), 0.0001, 0.01)
    w_in = centred(seeds[6], (F * E, H), (F * E) ** -0.5, 0.15625, ((1, 4),))
    b_in = centred(seeds[7], (H,), 0.5, 3.0, ((0, 4),))
    w_out = centred(seeds[8], (H,), 0.05, 0.29882812, ((0, 4),))
    return dict(owners=owners, local_rows=local_rows, weights=weights, labels=labels, table=table, accum=accum, w_in=w_in, b_in=b_in, w_out=w_out)


step_size = 0.5

def reference(owners, local_rows, weights, labels, table, accum, w_in, b_in, w_out):
    block_rows = math.gcd(SAMPLES, 1024)
    block_count = SAMPLES // block_rows
    row_ids = (owners * ROWS_DEV + local_rows).astype(jnp.int32)
    bias = b_in.astype(jnp.float32)
    out_proj = w_out.astype(jnp.float32)

    def accumulate(row_grad, blocks):
        block_ids, bag_weights, bag_labels = blocks
        looked = table[block_ids].astype(jnp.bfloat16)
        looked_f = looked.astype(jnp.float32)
        weight_sums = lax.optimization_barrier(jnp.sum(bag_weights, axis=-1))
        pooled = lax.optimization_barrier(jnp.sum(bag_weights[..., None] * looked_f, axis=2)) / weight_sums[..., None]
        inputs = pooled.astype(jnp.bfloat16).reshape(block_rows, F * E)
        preact = jnp.dot(inputs, w_in, preferred_element_type=jnp.float32) + bias
        sigma_pre = jax.nn.sigmoid(preact)
        logits = lax.optimization_barrier(jnp.sum(preact * sigma_pre * out_proj, axis=-1))
        logit_grad = jax.nn.sigmoid(logits) - bag_labels.astype(jnp.float32)
        slope = sigma_pre * (1.0 + preact * (1.0 - sigma_pre))
        dhidden = (logit_grad[:, None] * out_proj * slope).astype(jnp.bfloat16)
        dinputs = lax.dot_general(dhidden, w_in, (((1,), (1,)), ((), ())), preferred_element_type=jnp.float32)
        dpooled = dinputs.reshape(block_rows, F, E)
        along = lax.optimization_barrier(jnp.sum(looked_f * dpooled[:, :, None, :], axis=-1))
        centre = lax.optimization_barrier(jnp.sum(pooled * dpooled, axis=-1))
        weight_grads = (along - centre[..., None]) / weight_sums[..., None]
        slot_grad = ((bag_weights / weight_sums[..., None])[..., None] * dpooled[:, :, None, :]).astype(jnp.bfloat16)
        row_grad = row_grad.at[block_ids.reshape(-1)].add(slot_grad.reshape(-1, E).astype(jnp.float32))
        return (row_grad, weight_grads)
    start_grad = jnp.zeros((ROWS_DEV * N_OWNER, E), jnp.float32)
    row_grad, weight_grads = lax.scan(accumulate, start_grad, (row_ids.reshape(block_count, block_rows, F, L), weights.reshape(block_count, block_rows, F, L), labels.reshape(block_count, block_rows)))
    new_accum = accum + lax.optimization_barrier(jnp.mean(row_grad * row_grad, axis=-1))
    new_table = table - step_size * row_grad / jnp.sqrt(new_accum)[:, None]
    return (new_table, new_accum, weight_grads.reshape(SAMPLES, F, L))
```

```python
import functools

import jax
import jax.numpy as jnp
from jax import lax
from jax.experimental import pallas as pl
from jax.experimental.pallas import tpu as pltpu
from jax.sharding import PartitionSpec as P

step_size = 0.5
UNIQ = 104
ROWS_DEV = 2048
LANES = 128
VMEM_LIMIT = 56 * 1024 * 1024
f32, bf16, i32 = jnp.float32, jnp.bfloat16, jnp.int32


def dot(a, b, dims=((1,), (0,))):
    return lax.dot_general(a, b, (dims, ((), ())), preferred_element_type=f32)


def params(sem=None):
    return pltpu.CompilerParams(vmem_limit_bytes=VMEM_LIMIT, dimension_semantics=sem)


def index_kernel(own_ref, loc_ref, w_ref, list_ref, u_ref, c_ref):
    fields, bag_len, samples = own_ref.shape
    groups = u_ref.shape[0]
    his = ROWS_DEV // LANES
    lo_iota = lax.broadcasted_iota(i32, (LANES, samples), 0)
    hi_iota = lax.broadcasted_iota(i32, (his, samples), 0)

    def marks(row):
        lo = jnp.where(lo_iota == (row & (LANES - 1)), 1.0, 0.0).astype(bf16)
        hi = jnp.where(hi_iota == (row >> 7), 1.0, 0.0)
        return lo, hi

    count = jnp.zeros((his, LANES), f32)
    for f in range(fields):
        for j in range(bag_len):
            lo, hi = marks(loc_ref[f, j : j + 1, :])
            count = count + dot(hi.astype(bf16), lo, ((1,), (1,)))
    present = jnp.where(count > 0.5, 1.0, 0.0)
    tri = jnp.where(
        lax.broadcasted_iota(i32, (LANES, LANES), 0) <= lax.broadcasted_iota(i32, (LANES, LANES), 1), 1.0, 0.0
    ).astype(bf16)
    upto = dot(present.astype(bf16), tri)
    below = jnp.where(
        lax.broadcasted_iota(i32, (his, his), 0) > lax.broadcasted_iota(i32, (his, his), 1), 1.0, 0.0
    ).astype(bf16)
    totals = jnp.broadcast_to(upto[:, LANES - 1 :], (his, LANES))
    rank = upto - present + dot(below, totals.astype(bf16))
    rank_cols = jnp.where(present > 0.5, rank, -1.0).T
    lane = lax.broadcasted_iota(i32, (LANES, LANES), 1).astype(f32)
    sub = lax.broadcasted_iota(i32, (LANES, LANES), 0).astype(f32)
    listed = jnp.zeros((LANES, LANES), f32)
    for h in range(his):
        listed = listed + jnp.where(rank_cols[:, h : h + 1] == lane, sub + float(h * LANES), 0.0)
    list_ref[...] = jnp.sum(listed, axis=0, keepdims=True).astype(i32)

    rank_b = rank.astype(bf16)
    own_iota = lax.broadcasted_iota(i32, (groups, samples), 0)
    for f in range(fields):
        wsum = w_ref[f, 0:1, :]
        for j in range(1, bag_len):
            wsum = wsum + w_ref[f, j : j + 1, :]
        u_map = jnp.full((groups, samples), -1.0, f32)
        c_map = jnp.zeros((groups, samples), f32)
        for j in range(bag_len):
            lo, hi = marks(loc_ref[f, j : j + 1, :])
            u = jnp.sum(dot(rank_b, lo) * hi, axis=0, keepdims=True)
            here = own_iota == own_ref[f, j : j + 1, :]
            u_map = jnp.where(here, u, u_map)
            c_map = jnp.where(here, w_ref[f, j : j + 1, :] / wsum, c_map)
        u_ref[:, f * samples : (f + 1) * samples] = u_map
        c_ref[:, f * samples : (f + 1) * samples] = c_map


def index_call(own, loc, w, groups):
    fields, _, samples = own.shape
    bags = fields * samples
    return pl.pallas_call(
        index_kernel,
        out_shape=(
            jax.ShapeDtypeStruct((1, LANES), i32),
            jax.ShapeDtypeStruct((groups, bags), f32),
            jax.ShapeDtypeStruct((groups, bags), f32),
        ),
        compiler_params=params(),
    )(own, loc, w)


def take_kernel(list_ref, table_ref, out_ref, tb_ref):
    @pl.when(pl.program_id(0) == 0)
    def _():
        tb_ref[...] = table_ref[...].astype(bf16)

    n = list_ref.shape[1]
    rows = table_ref.shape[0]
    asked = jnp.broadcast_to(list_ref[...], (8, n)).T[:, :1]
    marks = jnp.where(lax.broadcasted_iota(i32, (n, rows), 1) == asked, 1.0, 0.0).astype(bf16)
    out_ref[...] = dot(marks, tb_ref[...]).astype(bf16)


def take_call(lists, table):
    n = lists.shape[1]
    rows, width = table.shape
    block = 512 if n % 512 == 0 else n
    return pl.pallas_call(
        take_kernel,
        grid=(n // block,),
        in_specs=[
            pl.BlockSpec((1, block), lambda i: (0, i)),
            pl.BlockSpec((rows, width), lambda i: (0, 0)),
        ],
        out_specs=pl.BlockSpec((block, width), lambda i: (i, 0)),
        out_shape=jax.ShapeDtypeStruct((n, width), bf16),
        scratch_shapes=[pltpu.VMEM((rows, width), bf16)],
        compiler_params=params(("arbitrary",)),
    )(lists, table)


def build(u_ref, c_ref, a_ref, fields, samples, per_step):
    iota = lax.broadcasted_iota(i32, (UNIQ, samples), 0).astype(f32)
    for f in range(fields):
        cols = slice(f * samples, (f + 1) * samples)
        for o in range(0, per_step, 2):
            pair = [
                jnp.where(iota == u_ref[o + k : o + k + 1, cols], c_ref[o + k : o + k + 1, cols], 0.0)
                for k in range(2)
            ]
            a_ref[o * UNIQ : (o + 2) * UNIQ, cols] = jnp.concatenate(pair, axis=0).astype(bf16)


def pool_kernel(fields, u_ref, c_ref, r_ref, x_ref, a_ref, acc_ref):
    per_step, bags = u_ref.shape
    samples = bags // fields
    width = r_ref.shape[1]

    @pl.when(pl.program_id(0) == 0)
    def _():
        acc_ref[...] = jnp.zeros_like(acc_ref)

    build(u_ref, c_ref, a_ref, fields, samples, per_step)
    rt = r_ref[...].astype(f32).T.astype(bf16)
    for f in range(fields):
        cols = slice(f * samples, (f + 1) * samples)
        acc_ref[:, cols] += dot(rt, a_ref[:, cols])

    @pl.when(pl.program_id(0) == pl.num_programs(0) - 1)
    def _():
        for f in range(fields):
            x_ref[:, f * width : (f + 1) * width] = acc_ref[:, f * samples : (f + 1) * samples].T.astype(bf16)


def pool_call(u, c, r, fields):
    groups, bags = u.shape
    width = r.shape[1]
    per_step = min(8, groups)
    return pl.pallas_call(
        functools.partial(pool_kernel, fields),
        grid=(groups // per_step,),
        in_specs=[
            pl.BlockSpec((per_step, bags), lambda i: (i, 0)),
            pl.BlockSpec((per_step, bags), lambda i: (i, 0)),
            pl.BlockSpec((per_step * UNIQ, width), lambda i: (i, 0)),
        ],
        out_specs=pl.BlockSpec((bags // fields, fields * width), lambda i: (0, 0)),
        out_shape=jax.ShapeDtypeStruct((bags // fields, fields * width), bf16),
        scratch_shapes=[
            pltpu.VMEM((per_step * UNIQ, bags), bf16),
            pltpu.VMEM((width, bags), f32),
        ],
        compiler_params=params(("arbitrary",)),
    )(u, c, r)


def head_kernel(x_ref, lab_ref, wa_ref, wb_ref, dt_ref, d_ref, pre_ref, acc_ref):
    samples, ins = x_ref.shape
    parts, _, cut = wa_ref.shape
    width = d_ref.shape[1]
    blocks = [(ref, p) for ref in (wa_ref, wb_ref) for p in range(parts)]
    x = x_ref[...]
    logits = jnp.zeros((samples, 1), f32)
    for k, (ref, p) in enumerate(blocks):
        pre = dot(x, ref[p, :ins, :]) + ref[p, ins : ins + 1, :].astype(f32)
        pre_ref[k] = pre
        out = ref[p, ins + 1 : ins + 2, :].astype(f32)
        logits = logits + jnp.sum(pre * jax.nn.sigmoid(pre) * out, axis=1, keepdims=True)
    labels = jnp.broadcast_to(lab_ref[...], (8, samples)).T[:, :1]
    grad = jax.nn.sigmoid(logits) - labels
    for k, (ref, p) in enumerate(blocks):
        pre = pre_ref[k]
        sig = jax.nn.sigmoid(pre)
        out = ref[p, ins + 1 : ins + 2, :].astype(f32)
        dh = (grad * out * (sig * (1.0 + pre * (1.0 - sig)))).astype(bf16)
        part = dot(ref[p, :ins, :], dh, ((1,), (1,)))
        acc_ref[...] = part if k == 0 else acc_ref[...] + part
    for f in range(ins // width):
        block = acc_ref[f * width : (f + 1) * width, :]
        dt_ref[f * width : (f + 1) * width, :] = block.astype(bf16)
        d_ref[f * samples : (f + 1) * samples, :] = block.T.astype(bf16)


def head_call(x, labels, wa, wb, width):
    samples, ins = x.shape
    parts, _, cut = wa.shape
    return pl.pallas_call(
        head_kernel,
        out_shape=(
            jax.ShapeDtypeStruct((ins, samples), bf16),
            jax.ShapeDtypeStruct((ins // width * samples, width), bf16),
        ),
        scratch_shapes=[
            pltpu.VMEM((2 * parts, samples, cut), f32),
            pltpu.VMEM((ins, samples), f32),
        ],
        compiler_params=params(),
    )(x, labels, wa, wb)


def give_kernel(fields, u_ref, c_ref, d_ref, g_ref, a_ref):
    per_step, bags = u_ref.shape
    build(u_ref, c_ref, a_ref, fields, bags // fields, per_step)
    g_ref[...] = dot(a_ref[...], d_ref[...]).astype(bf16)


def give_call(u, c, d, fields):
    groups, bags = u.shape
    width = d.shape[1]
    per_step = min(8, groups)
    return pl.pallas_call(
        functools.partial(give_kernel, fields),
        grid=(groups // per_step,),
        in_specs=[
            pl.BlockSpec((per_step, bags), lambda i: (i, 0)),
            pl.BlockSpec((per_step, bags), lambda i: (i, 0)),
            pl.BlockSpec((bags, width), lambda i: (0, 0)),
        ],
        out_specs=pl.BlockSpec((per_step * UNIQ, width), lambda i: (i, 0)),
        out_shape=jax.ShapeDtypeStruct((groups * UNIQ, width), bf16),
        scratch_shapes=[pltpu.VMEM((per_step * UNIQ, bags), bf16)],
        compiler_params=params(("arbitrary",)),
    )(u, c, d)


def along_kernel(own_ref, w_ref, u_ref, r_ref, dt_ref, out_ref, acc_ref):
    fields, bag_len, samples = own_ref.shape
    per_step = u_ref.shape[0]
    width = r_ref.shape[1]
    step = pl.program_id(0)

    @pl.when(step == 0)
    def _():
        acc_ref[...] = jnp.zeros_like(acc_ref)

    iota = lax.broadcasted_iota(i32, (UNIQ, samples), 0).astype(f32)
    for f in range(fields):
        cols = slice(f * samples, (f + 1) * samples)
        prod = dot(r_ref[...], dt_ref[f * width : (f + 1) * width, :])
        own = own_ref[f]
        got = acc_ref[f]
        for o in range(per_step):
            hit = jnp.where(iota == u_ref[o : o + 1, cols], prod[o * UNIQ : (o + 1) * UNIQ, :], 0.0)
            value = jnp.sum(hit, axis=0, keepdims=True)
            got = jnp.where(own == step * per_step + o, value, got)
        acc_ref[f] = got

    @pl.when(step == pl.num_programs(0) - 1)
    def _():
        for f in range(fields):
            w = w_ref[f]
            wsum = jnp.sum(w, axis=0, keepdims=True)
            along = acc_ref[f]
            centre = jnp.sum(w * along, axis=0, keepdims=True) / wsum
            out_ref[f] = (along - centre) / wsum


def along_call(own, w, u, r, dt):
    groups, bags = u.shape
    width = r.shape[1]
    per_step = min(8, groups)
    whole3 = pl.BlockSpec(own.shape, lambda i: (0, 0, 0))
    return pl.pallas_call(
        along_kernel,
        grid=(groups // per_step,),
        in_specs=[
            whole3,
            whole3,
            pl.BlockSpec((per_step, bags), lambda i: (i, 0)),
            pl.BlockSpec((per_step * UNIQ, width), lambda i: (i, 0)),
            pl.BlockSpec(dt.shape, lambda i: (0, 0)),
        ],
        out_specs=whole3,
        out_shape=jax.ShapeDtypeStruct(own.shape, f32),
        scratch_shapes=[pltpu.VMEM(own.shape, f32)],
        compiler_params=params(("arbitrary",)),
    )(own, w, u, r, dt)


def add_kernel(list_ref, g_ref, out_ref, acc_ref):
    rows = out_ref.shape[0]
    n = list_ref.shape[1]
    marks = jnp.where(lax.broadcasted_iota(i32, (rows, n), 0) == list_ref[...], 1.0, 0.0).astype(bf16)
    part = dot(marks, g_ref[...])

    @pl.when(pl.program_id(0) == 0)
    def _():
        acc_ref[...] = part

    @pl.when(pl.program_id(0) > 0)
    def _():
        acc_ref[...] += part

    @pl.when(pl.program_id(0) == pl.num_programs(0) - 1)
    def _():
        out_ref[...] = acc_ref[...].astype(bf16)


def add_call(lists, g, rows):
    n = lists.shape[1]
    width = g.shape[1]
    block = 512 if n % 512 == 0 else n
    return pl.pallas_call(
        add_kernel,
        grid=(n // block,),
        in_specs=[
            pl.BlockSpec((1, block), lambda i: (0, i)),
            pl.BlockSpec((block, width), lambda i: (i, 0)),
        ],
        out_specs=pl.BlockSpec((rows, width), lambda i: (0, 0)),
        out_shape=jax.ShapeDtypeStruct((rows, width), bf16),
        scratch_shapes=[pltpu.VMEM((rows, width), f32)],
        compiler_params=params(("arbitrary",)),
    )(lists, g)


def local(owners, local_rows, weights, labels, table, accum, w_in, b_in, w_out):
    samples, fields, bag_len = owners.shape
    rows, width = table.shape
    groups = lax.axis_size("owner")
    dense = lax.axis_size("dense")

    core = lax.axis_index("owner") % 2
    half = w_in.shape[1] // 2
    tail = jnp.zeros((14, w_in.shape[1]), bf16)
    head = jnp.concatenate([w_in, b_in[None], w_out[None], tail], axis=0)
    mine = lax.dynamic_slice_in_dim(head, core * half, half, axis=1)
    wa = lax.all_gather(mine, "dense", axis=0, tiled=False)
    wb = lax.ppermute(wa, "owner", [(i, i ^ 1) for i in range(groups)])

    own = owners.transpose(1, 2, 0)
    w = weights.transpose(1, 2, 0)
    listed, u, c = index_call(own, local_rows.transpose(1, 2, 0), w, groups)
    lists = lax.all_gather(listed[0, :UNIQ], "owner", axis=0, tiled=True)[None]
    found = take_call(lists, table)
    r = lax.all_to_all(found.reshape(groups, UNIQ, width), "owner", split_axis=0, concat_axis=0, tiled=True)
    r = r.reshape(groups * UNIQ, width)
    x = pool_call(u, c, r, fields)
    dt, d = head_call(x, labels.astype(f32)[None], wa, wb, width)
    g = give_call(u, c, d, fields)
    got = lax.all_to_all(g.reshape(groups, UNIQ, width), "owner", split_axis=0, concat_axis=0, tiled=True)
    weight_grad = along_call(own, w, u, r, dt).transpose(2, 0, 1)
    part = add_call(lists, got.reshape(groups * UNIQ, width), rows)
    pieces = lax.all_to_all(part.reshape(dense, rows // dense, width), "dense", split_axis=0, concat_axis=0, tiled=True)
    summed = jnp.sum(pieces.astype(f32), axis=0).astype(bf16)
    row_grad = lax.all_gather(summed, "dense", axis=0, tiled=True).astype(f32)
    new_accum = accum + jnp.mean(row_grad * row_grad, axis=-1)
    new_table = table - step_size * row_grad / jnp.sqrt(new_accum)[:, None]
    return (new_table, new_accum, weight_grad)


def solution(mesh):
    placed = (
        P(("owner", "dense"), None, None),
        P(("owner", "dense"), None, None),
        P(("owner", "dense"), None, None),
        P(("owner", "dense")),
        P("owner", None),
        P("owner"),
        P(None, "dense"),
        P("dense"),
        P("dense"),
    )
    return jax.shard_map(
        local,
        mesh=mesh,
        in_specs=placed,
        out_specs=(P("owner", None), P("owner"), P(("owner", "dense"), None, None)),
        check_vma=False,
    )
```

```python
import functools

import jax
import jax.numpy as jnp
from jax import lax
from jax.experimental import pallas as pl
from jax.experimental.pallas import tpu as pltpu
from jax.sharding import PartitionSpec as P

step_size = 0.5
UNIQ = 104
ROWS_DEV = 2048
LANES = 128
CHUNKS = ((0, 48), (48, 104))
TAIL = 16
VMEM_LIMIT = 56 * 1024 * 1024
f32, bf16, i32 = jnp.float32, jnp.bfloat16, jnp.int32


def dot(a, b, dims=((1,), (0,))):
    return lax.dot_general(a, b, (dims, ((), ())), preferred_element_type=f32)


def params(sem=None):
    return pltpu.CompilerParams(vmem_limit_bytes=VMEM_LIMIT, dimension_semantics=sem)


def cost(flops, moved=1 << 20):
    return pl.CostEstimate(flops=1 << 20, bytes_accessed=1 << 10, transcendentals=0)


def after(x, *before):
    return lax.optimization_barrier((x, *before))[0]


def marks_of(row, samples):
    lo = lax.broadcasted_iota(i32, (LANES, samples), 0) == (row & (LANES - 1))
    hi = lax.broadcasted_iota(i32, (ROWS_DEV // LANES, samples), 0) == (row >> 7)
    return jnp.where(lo, 1.0, 0.0).astype(bf16), jnp.where(hi, 1.0, 0.0)


def list_kernel(loc_ref, list_ref, rank_ref):
    fields, bag_len, samples = loc_ref.shape
    his = ROWS_DEV // LANES
    count = jnp.zeros((his, LANES), f32)
    for f in range(fields):
        for j in range(bag_len):
            lo, hi = marks_of(loc_ref[f, j : j + 1, :], samples)
            count = count + dot(hi.astype(bf16), lo, ((1,), (1,)))
    present = jnp.where(count > 0.5, 1.0, 0.0)
    tri = jnp.where(
        lax.broadcasted_iota(i32, (LANES, LANES), 0) <= lax.broadcasted_iota(i32, (LANES, LANES), 1), 1.0, 0.0
    ).astype(bf16)
    upto = dot(present.astype(bf16), tri)
    below = jnp.where(
        lax.broadcasted_iota(i32, (his, his), 0) > lax.broadcasted_iota(i32, (his, his), 1), 1.0, 0.0
    ).astype(bf16)
    totals = jnp.broadcast_to(upto[:, LANES - 1 :], (his, LANES))
    rank = upto - present + dot(below, totals.astype(bf16))
    rank_ref[...] = rank
    rank_cols = jnp.where(present > 0.5, rank, -1.0).T
    lane = lax.broadcasted_iota(i32, (LANES, LANES), 1).astype(f32)
    sub = lax.broadcasted_iota(i32, (LANES, LANES), 0).astype(f32)
    listed = jnp.zeros((LANES, LANES), f32)
    for h in range(his):
        listed = listed + jnp.where(rank_cols[:, h : h + 1] == lane, sub + float(h * LANES), 0.0)
    row = jnp.sum(listed, axis=0, keepdims=True).astype(i32)
    list_ref[...] = jnp.broadcast_to(row, list_ref.shape)


def list_call(loc, groups):
    return pl.pallas_call(
        list_kernel,
        out_shape=(
            jax.ShapeDtypeStruct((groups, LANES), i32),
            jax.ShapeDtypeStruct((ROWS_DEV // LANES, LANES), f32),
        ),
        compiler_params=params(),
        cost_estimate=cost(1 << 31),
    )(loc)


def map_kernel(own_ref, loc_ref, w_ref, rank_ref, u_ref, c_ref):
    fields, bag_len, samples = own_ref.shape
    groups = u_ref.shape[0]
    rank_b = rank_ref[...].astype(bf16)
    own_iota = lax.broadcasted_iota(i32, (groups, samples), 0)
    for f in range(fields):
        wsum = w_ref[f, 0:1, :]
        for j in range(1, bag_len):
            wsum = wsum + w_ref[f, j : j + 1, :]
        u_map = jnp.full((groups, samples), -1.0, f32)
        c_map = jnp.zeros((groups, samples), f32)
        for j in range(bag_len):
            lo, hi = marks_of(loc_ref[f, j : j + 1, :], samples)
            u = jnp.sum(dot(rank_b, lo) * hi, axis=0, keepdims=True)
            here = own_iota == own_ref[f, j : j + 1, :]
            u_map = jnp.where(here, u, u_map)
            c_map = jnp.where(here, w_ref[f, j : j + 1, :] / wsum, c_map)
        u_ref[:, f * samples : (f + 1) * samples] = u_map
        c_ref[:, f * samples : (f + 1) * samples] = c_map


def map_call(own, loc, w, rank, groups):
    fields, _, samples = own.shape
    bags = fields * samples
    return pl.pallas_call(
        map_kernel,
        out_shape=(
            jax.ShapeDtypeStruct((groups, bags), f32),
            jax.ShapeDtypeStruct((groups, bags), f32),
        ),
        compiler_params=params(),
        cost_estimate=cost(1 << 31),
    )(own, loc, w, rank)


def half_kernel(core_ref, w_ref, b_ref, o_ref, out_ref):
    ins = w_ref.shape[0]
    out_ref[:ins, :] = w_ref[...]
    cut = w_ref.shape[1]
    rows = jnp.concatenate(
        [b_ref[...].astype(f32), o_ref[...].astype(f32), jnp.zeros((TAIL - 2, cut), f32)], axis=0
    )
    out_ref[ins:, :] = rows.astype(bf16)


def half_call(core, w_in, b_in, w_out):
    ins, hidden = w_in.shape
    cut = hidden // 2
    return pl.pallas_call(
        half_kernel,
        grid_spec=pltpu.PrefetchScalarGridSpec(
            num_scalar_prefetch=1,
            grid=(1,),
            in_specs=[
                pl.BlockSpec((ins, cut), lambda i, core: (0, core[0])),
                pl.BlockSpec((1, cut), lambda i, core: (0, core[0])),
                pl.BlockSpec((1, cut), lambda i, core: (0, core[0])),
            ],
            out_specs=pl.BlockSpec((ins + TAIL, cut), lambda i, core: (0, 0)),
        ),
        out_shape=jax.ShapeDtypeStruct((ins + TAIL, cut), bf16),
        compiler_params=params(("arbitrary",)),
    )(core, w_in, b_in[None], w_out[None])


def take_kernel(lo, hi, list_ref, tb_ref, out_ref):
    rows = tb_ref.shape[0]
    per_step = list_ref.shape[0]
    asked = list_ref[...].T
    iota = lax.broadcasted_iota(i32, (hi - lo, rows), 1)
    marks = [jnp.where(iota == asked[lo:hi, o : o + 1], 1.0, 0.0) for o in range(per_step)]
    out_ref[...] = dot(jnp.concatenate(marks, axis=0).astype(bf16), tb_ref[...]).astype(bf16)


def take_call(lists, tb, lo, hi):
    groups = lists.shape[0]
    rows, width = tb.shape
    per_step = min(8, groups)
    n = hi - lo
    return pl.pallas_call(
        functools.partial(take_kernel, lo, hi),
        grid=(groups // per_step,),
        in_specs=[
            pl.BlockSpec((per_step, LANES), lambda i: (i, 0)),
            pl.BlockSpec((rows, width), lambda i: (0, 0)),
        ],
        out_specs=pl.BlockSpec((per_step * n, width), lambda i: (i, 0)),
        out_shape=jax.ShapeDtypeStruct((groups * n, width), bf16),
        compiler_params=params(("arbitrary",)),
        cost_estimate=cost(2 * groups * n * rows * width * 2),
    )(lists, tb)


def build(u_ref, c_ref, a_ref, fields, samples, per_step, lo, hi):
    n = hi - lo
    iota = lax.broadcasted_iota(i32, (n, samples), 0).astype(f32) + float(lo)
    for f in range(fields):
        cols = slice(f * samples, (f + 1) * samples)
        for o in range(0, per_step, 2):
            pair = [
                jnp.where(iota == u_ref[o + k : o + k + 1, cols], c_ref[o + k : o + k + 1, cols], 0.0)
                for k in range(2)
            ]
            a_ref[o * n : (o + 2) * n, cols] = jnp.concatenate(pair, axis=0).astype(bf16)


def pool_kernel(fields, lo, hi, last, u_ref, c_ref, r_ref, *refs):
    per_step, bags = u_ref.shape
    samples = bags // fields
    width = r_ref.shape[1]
    prev_ref = refs[0] if last else None
    x_ref, a_ref, acc_ref = refs[-3:] if last else (None, refs[-1], refs[0])

    @pl.when(pl.program_id(0) == 0)
    def _():
        acc_ref[...] = prev_ref[...] if last else jnp.zeros_like(acc_ref)

    build(u_ref, c_ref, a_ref, fields, samples, per_step, lo, hi)
    rt = r_ref[...].astype(f32).T.astype(bf16)
    for f in range(fields):
        cols = slice(f * samples, (f + 1) * samples)
        acc_ref[:, cols] += dot(rt, a_ref[:, cols])

    if last:

        @pl.when(pl.program_id(0) == pl.num_programs(0) - 1)
        def _():
            for f in range(fields):
                x_ref[:, f * width : (f + 1) * width] = acc_ref[:, f * samples : (f + 1) * samples].T.astype(bf16)


def pool_call(u, c, r, fields, lo, hi, prev, last):
    groups, bags = u.shape
    width = r.shape[1]
    per_step = min(8, groups)
    n = hi - lo
    acc = jax.ShapeDtypeStruct((width, bags), f32)
    x = jax.ShapeDtypeStruct((bags // fields, fields * width), bf16)
    acc_spec = pl.BlockSpec((width, bags), lambda i: (0, 0))
    return pl.pallas_call(
        functools.partial(pool_kernel, fields, lo, hi, last),
        grid=(groups // per_step,),
        in_specs=[
            pl.BlockSpec((per_step, bags), lambda i: (i, 0)),
            pl.BlockSpec((per_step, bags), lambda i: (i, 0)),
            pl.BlockSpec((per_step * n, width), lambda i: (i, 0)),
        ]
        + ([acc_spec] if last else []),
        out_specs=pl.BlockSpec(x.shape, lambda i: (0, 0)) if last else acc_spec,
        out_shape=x if last else acc,
        scratch_shapes=[pltpu.VMEM((per_step * n, bags), bf16)] + ([pltpu.VMEM((width, bags), f32)] if last else []),
        compiler_params=params(("arbitrary",)),
        cost_estimate=cost(2 * groups * n * bags * width * 2),
    )(u, c, r, *([prev] if last else []))


def head_kernel(sides, x_ref, lab_ref, *refs):
    weights, (dt_ref, d_ref, pre_ref, acc_ref), refs = refs[: 5 * sides], refs[5 * sides : 5 * sides + 4], refs[5 * sides + 4 :]
    held, sem = refs[: 5 * sides], refs[5 * sides]
    samples, ins = x_ref.shape
    width = d_ref.shape[1]
    copies = [pltpu.make_async_copy(weights[k], held[k], sem.at[k]) for k in range(5 * sides)]
    for copy in copies:
        copy.start()
    x = x_ref[...]
    top = held[3].shape[0]
    logits = jnp.zeros((samples, 1), f32)
    blocks = [(5 * s + p,) for s in range(sides) for p in range(3)] + [(5 * s + 3, 5 * s + 4) for s in range(sides)]

    def tail(block):
        ref = held[block[-1]]
        at = ins if len(block) == 1 else ins - top
        return ref[at : at + 1, :].astype(f32), ref[at + 1 : at + 2, :].astype(f32)

    for k, block in enumerate(blocks):
        for b in block:
            copies[b].wait()
        bias, out = tail(block)
        if len(block) == 1:
            pre = dot(x, held[block[0]][:ins, :]) + bias
        else:
            pre = dot(x[:, :top], held[block[0]][...]) + dot(x[:, top:], held[block[1]][: ins - top, :]) + bias
        pre_ref[k] = pre
        logits = logits + jnp.sum(pre * jax.nn.sigmoid(pre) * out, axis=1, keepdims=True)
    labels = jnp.broadcast_to(lab_ref[...], (8, samples)).T[:, :1]
    grad = jax.nn.sigmoid(logits) - labels
    for k, block in enumerate(blocks):
        pre = pre_ref[k]
        sig = jax.nn.sigmoid(pre)
        out = tail(block)[1]
        dh = (grad * out * (sig * (1.0 + pre * (1.0 - sig)))).astype(bf16)
        if len(block) == 1:
            part = dot(held[block[0]][:ins, :], dh, ((1,), (1,)))
            acc_ref[...] = part if k == 0 else acc_ref[...] + part
        else:
            acc_ref[:top, :] += dot(held[block[0]][...], dh, ((1,), (1,)))
            acc_ref[top:, :] += dot(held[block[1]][: ins - top, :], dh, ((1,), (1,)))
    for f in range(ins // width):
        block = acc_ref[f * width : (f + 1) * width, :]
        dt_ref[f * width : (f + 1) * width, :] = block.astype(bf16)
        d_ref[f * samples : (f + 1) * samples, :] = block.T.astype(bf16)


def head_call(x, labels, weights, width):
    samples, ins = x.shape
    sides = len(weights) // 5
    cut = weights[0].shape[1]
    n = len(weights)
    vmem = pl.BlockSpec(memory_space=pltpu.VMEM)
    return pl.pallas_call(
        functools.partial(head_kernel, sides),
        in_specs=[vmem, vmem] + [pl.BlockSpec(memory_space=pl.ANY)] * n,
        out_specs=(vmem, vmem),
        out_shape=(
            jax.ShapeDtypeStruct((ins, samples), bf16),
            jax.ShapeDtypeStruct((ins // width * samples, width), bf16),
        ),
        scratch_shapes=[
            pltpu.VMEM((4 * sides, samples, cut), f32),
            pltpu.VMEM((ins, samples), f32),
        ]
        + [pltpu.VMEM(a.shape, bf16) for a in weights]
        + [pltpu.SemaphoreType.DMA((n,))],
        compiler_params=params(),
        cost_estimate=cost(4 * samples * ins * cut * 4 * sides, 14 << 20),
    )(x, labels, *weights)


def give_kernel(fields, lo, hi, u_ref, c_ref, d_ref, g_ref, a_ref):
    per_step, bags = u_ref.shape
    build(u_ref, c_ref, a_ref, fields, bags // fields, per_step, lo, hi)
    g_ref[...] = dot(a_ref[...], d_ref[...]).astype(bf16)


def give_call(u, c, d, fields, lo, hi):
    groups, bags = u.shape
    width = d.shape[1]
    per_step = min(8, groups)
    n = hi - lo
    return pl.pallas_call(
        functools.partial(give_kernel, fields, lo, hi),
        grid=(groups // per_step,),
        in_specs=[
            pl.BlockSpec((per_step, bags), lambda i: (i, 0)),
            pl.BlockSpec((per_step, bags), lambda i: (i, 0)),
            pl.BlockSpec((bags, width), lambda i: (0, 0)),
        ],
        out_specs=pl.BlockSpec((per_step * n, width), lambda i: (i, 0)),
        out_shape=jax.ShapeDtypeStruct((groups * n, width), bf16),
        scratch_shapes=[pltpu.VMEM((per_step * n, bags), bf16)],
        compiler_params=params(("arbitrary",)),
        cost_estimate=cost(2 * groups * n * bags * width * 2),
    )(u, c, d)


def along_kernel(own_ref, w_ref, u_ref, dt_ref, *refs):
    r_refs, (out_ref, acc_ref) = refs[:-2], refs[-2:]
    fields, bag_len, samples = own_ref.shape
    per_step = u_ref.shape[0]
    width = r_refs[0].shape[1]
    step = pl.program_id(0)

    @pl.when(step == 0)
    def _():
        acc_ref[...] = jnp.zeros_like(acc_ref)

    for f in range(fields):
        cols = slice(f * samples, (f + 1) * samples)
        d = dt_ref[f * width : (f + 1) * width, :]
        prods = [dot(r_ref[...], d) for r_ref in r_refs]
        own = own_ref[f]
        got = acc_ref[f]
        for o in range(per_step):
            value = None
            for (lo, hi), prod in zip(CHUNKS, prods):
                n = hi - lo
                iota = lax.broadcasted_iota(i32, (n, samples), 0).astype(f32) + float(lo)
                hit = jnp.where(iota == u_ref[o : o + 1, cols], prod[o * n : (o + 1) * n, :], 0.0)
                part = jnp.sum(hit.reshape(n // 8, 8, samples), axis=0)
                value = part if value is None else value + part
            value = jnp.sum(value, axis=0, keepdims=True)
            got = jnp.where(own == step * per_step + o, value, got)
        acc_ref[f] = got

    @pl.when(step == pl.num_programs(0) - 1)
    def _():
        for f in range(fields):
            w = w_ref[f]
            wsum = jnp.sum(w, axis=0, keepdims=True)
            along = acc_ref[f]
            centre = jnp.sum(w * along, axis=0, keepdims=True) / wsum
            out_ref[f] = (along - centre) / wsum


def along_call(own, w, u, dt, rs):
    groups, bags = u.shape
    width = rs[0].shape[1]
    per_step = min(8, groups)
    whole3 = pl.BlockSpec(own.shape, lambda i: (0, 0, 0))
    return pl.pallas_call(
        along_kernel,
        grid=(groups // per_step,),
        in_specs=[
            whole3,
            whole3,
            pl.BlockSpec((per_step, bags), lambda i: (i, 0)),
            pl.BlockSpec(dt.shape, lambda i: (0, 0)),
        ]
        + [pl.BlockSpec((per_step * (hi - lo), width), lambda i: (i, 0)) for lo, hi in CHUNKS],
        out_specs=whole3,
        out_shape=jax.ShapeDtypeStruct(own.shape, f32),
        scratch_shapes=[pltpu.VMEM(own.shape, f32)],
        compiler_params=params(("arbitrary",)),
        cost_estimate=cost(2 * groups * UNIQ * bags * width * 2),
    )(own, w, u, dt, *rs)


def add_kernel(last, list_ref, g_ref, *refs):
    prev_ref = refs[0] if last else None
    out_ref, acc_ref = refs[-2:] if last else (None, refs[0])
    rows = acc_ref.shape[0]
    n = list_ref.shape[1]

    @pl.when(pl.program_id(0) == 0)
    def _():
        acc_ref[...] = prev_ref[...] if last else jnp.zeros_like(acc_ref)

    marks = jnp.where(lax.broadcasted_iota(i32, (rows, n), 0) == list_ref[...], 1.0, 0.0).astype(bf16)
    acc_ref[...] += dot(marks, g_ref[...])

    if last:

        @pl.when(pl.program_id(0) == pl.num_programs(0) - 1)
        def _():
            out_ref[...] = acc_ref[...].astype(bf16)


def add_call(lists, g, rows, prev, last):
    n = lists.shape[1]
    width = g.shape[1]
    block = 512 if n % 512 == 0 else n
    whole = pl.BlockSpec((rows, width), lambda i: (0, 0))
    return pl.pallas_call(
        functools.partial(add_kernel, last),
        grid=(n // block,),
        in_specs=[
            pl.BlockSpec((1, block), lambda i: (0, i)),
            pl.BlockSpec((block, width), lambda i: (i, 0)),
        ]
        + ([whole] if last else []),
        out_specs=whole,
        out_shape=jax.ShapeDtypeStruct((rows, width), bf16 if last else f32),
        scratch_shapes=[pltpu.VMEM((rows, width), f32)] if last else [],
        compiler_params=params(("arbitrary",)),
        cost_estimate=cost(2 * n * rows * width * 2),
    )(lists, g, *([prev] if last else []))


def send(x, groups):
    width = x.shape[1]
    return lax.all_to_all(
        x.reshape(groups, -1, width), "owner", split_axis=0, concat_axis=0, tiled=True
    ).reshape(-1, width)


def turn(x, shift):
    dense = lax.axis_size("dense")
    return lax.ppermute(x, "dense", [(i, (i + shift) % dense) for i in range(dense)])


def swap(x):
    return lax.ppermute(x, "owner", [(i, i ^ 1) for i in range(lax.axis_size("owner"))])


def local(owners, local_rows, weights, labels, table, accum, w_in, b_in, w_out):
    fields = owners.shape[1]
    rows, width = table.shape
    groups = lax.axis_size("owner")
    dense = lax.axis_size("dense")
    own, loc, w = (a.transpose(1, 2, 0) for a in (owners, local_rows, weights))

    mine = half_call((lax.axis_index("owner") % 2).astype(i32)[None], w_in, b_in, w_out)
    ahead, behind = turn(mine, 1), turn(mine, dense - 1)

    listed, rank = list_call(loc, groups)
    lists = lax.all_to_all(listed, "owner", split_axis=0, concat_axis=0, tiled=True)
    u, c = map_call(own, loc, w, rank, groups)
    flat = [lists[:, lo:hi].reshape(1, groups * (hi - lo)) for lo, hi in CHUNKS]
    tb = table.astype(bf16)

    found = [take_call(lists, tb, lo, hi) for lo, hi in CHUNKS]
    rs = [send(x, groups) for x in found]

    cut = (mine.shape[0] // 32) * 16
    ahead, behind = after(ahead, found[-1]), after(behind, found[-1])
    far = [turn(ahead[:cut], 1), turn(behind[cut:], dense - 1)]
    near = [mine, ahead, behind]
    other = [swap(after(a, found[-1])) for a in near]
    far = [after(a, rs[0]) for a in far]
    head_weights = near + far + other + [swap(a) for a in far]

    x = None
    for k, (lo, hi) in enumerate(CHUNKS):
        x = pool_call(u, c, rs[k], fields, lo, hi, x, k == len(CHUNKS) - 1)
    dt, d = head_call(x, labels.astype(f32)[None], head_weights, width)
    gs = [give_call(u, c, d, fields, lo, hi) for lo, hi in CHUNKS]
    gots = [send(g, groups) for g in gs]
    weight_grad = along_call(own, w, u, after(dt, *gs), rs)
    part = None
    for k in range(len(CHUNKS)):
        got = after(gots[k], weight_grad) if k == 0 else gots[k]
        part = add_call(flat[k], got, rows, part, k == len(CHUNKS) - 1)

    cut = rows // dense
    me = lax.axis_index("dense")
    piece = lambda k: lax.dynamic_slice_in_dim(part, lax.rem(me + k, dense) * cut, cut, axis=0)
    total = piece(0).astype(f32)
    for k in range(1, dense):
        total = total + turn(piece(k), k).astype(f32)
    total = total.astype(bf16)
    row_grad = jnp.zeros((rows, width), bf16)
    for k in range(dense):
        got = total if k == 0 else turn(total, k)
        row_grad = lax.dynamic_update_slice_in_dim(row_grad, got, lax.rem(me + dense - k, dense) * cut, axis=0)
    row_grad = row_grad.astype(f32)
    new_accum = accum + jnp.mean(row_grad * row_grad, axis=-1)
    new_table = table - step_size * row_grad / jnp.sqrt(new_accum)[:, None]
    return (new_table, new_accum, weight_grad.transpose(2, 0, 1))


def solution(mesh):
    placed = (
        P(("owner", "dense"), None, None),
        P(("owner", "dense"), None, None),
        P(("owner", "dense"), None, None),
        P(("owner", "dense")),
        P("owner", None),
        P("owner"),
        P(None, "dense"),
        P("dense"),
        P("dense"),
    )
    return jax.shard_map(
        local,
        mesh=mesh,
        in_specs=placed,
        out_specs=(P("owner", None), P("owner"), P(("owner", "dense"), None, None)),
        check_vma=False,
    )
```

```python
import functools

import jax
import jax.numpy as jnp
from jax import lax
from jax.experimental import pallas as pl
from jax.experimental.pallas import tpu as pltpu
from jax.sharding import PartitionSpec as P

step_size = 0.5
UNIQ = 104
ROWS_DEV = 2048
LANES = 128
CHUNKS = ((0, 104),)
TAIL = 16
TAKE_BLOCK, POOL_STEP, GIVE_STEP, ADD_STEP, ALONG_STEP = 3328, 32, 32, 32, 8
VMEM_LIMIT = 56 * 1024 * 1024
f32, bf16, i32 = jnp.float32, jnp.bfloat16, jnp.int32


def dot(a, b, dims=((1,), (0,))):
    return lax.dot_general(a, b, (dims, ((), ())), preferred_element_type=f32)


def params(sem=None):
    return pltpu.CompilerParams(vmem_limit_bytes=VMEM_LIMIT, dimension_semantics=sem)


def cost(flops, moved=1 << 20):
    return pl.CostEstimate(flops=1 << 20, bytes_accessed=1 << 10, transcendentals=0)


def after(x, *before):
    return lax.optimization_barrier((x, *before))[0]


def marks_of(row, samples):
    lo = lax.broadcasted_iota(i32, (LANES, samples), 0) == (row & (LANES - 1))
    hi = lax.broadcasted_iota(i32, (ROWS_DEV // LANES, samples), 0) == (row >> 7)
    return jnp.where(lo, 1.0, 0.0).astype(bf16), jnp.where(hi, 1.0, 0.0)


def list_kernel(loc_ref, list_ref, rank_ref):
    fields, bag_len, samples = loc_ref.shape
    his = ROWS_DEV // LANES
    count = jnp.zeros((his, LANES), f32)
    for f in range(fields):
        for j in range(bag_len):
            lo, hi = marks_of(loc_ref[f, j : j + 1, :], samples)
            count = count + dot(hi.astype(bf16), lo, ((1,), (1,)))
    present = jnp.where(count > 0.5, 1.0, 0.0)
    tri = jnp.where(
        lax.broadcasted_iota(i32, (LANES, LANES), 0) <= lax.broadcasted_iota(i32, (LANES, LANES), 1), 1.0, 0.0
    ).astype(bf16)
    upto = dot(present.astype(bf16), tri)
    below = jnp.where(
        lax.broadcasted_iota(i32, (his, his), 0) > lax.broadcasted_iota(i32, (his, his), 1), 1.0, 0.0
    ).astype(bf16)
    totals = jnp.broadcast_to(upto[:, LANES - 1 :], (his, LANES))
    rank = upto - present + dot(below, totals.astype(bf16))
    rank_ref[...] = rank
    rank_cols = jnp.where(present > 0.5, rank, -1.0).T
    lane = lax.broadcasted_iota(i32, (LANES, LANES), 1).astype(f32)
    sub = lax.broadcasted_iota(i32, (LANES, LANES), 0).astype(f32)
    listed = jnp.zeros((LANES, LANES), f32)
    for h in range(his):
        listed = listed + jnp.where(rank_cols[:, h : h + 1] == lane, sub + float(h * LANES), 0.0)
    row = jnp.sum(listed, axis=0, keepdims=True).astype(i32)
    list_ref[...] = jnp.broadcast_to(row, list_ref.shape)


def list_call(loc, groups):
    return pl.pallas_call(
        list_kernel,
        out_shape=(
            jax.ShapeDtypeStruct((groups, LANES), i32),
            jax.ShapeDtypeStruct((ROWS_DEV // LANES, LANES), f32),
        ),
        compiler_params=params(),
        cost_estimate=cost(1 << 31),
    )(loc)


def map_kernel(own_ref, loc_ref, w_ref, rank_ref, u_ref, c_ref):
    fields, bag_len, samples = own_ref.shape
    groups = u_ref.shape[0]
    rank_b = rank_ref[...].astype(bf16)
    own_iota = lax.broadcasted_iota(i32, (groups, samples), 0)
    for f in range(fields):
        wsum = w_ref[f, 0:1, :]
        for j in range(1, bag_len):
            wsum = wsum + w_ref[f, j : j + 1, :]
        u_map = jnp.full((groups, samples), -1.0, f32)
        c_map = jnp.zeros((groups, samples), f32)
        for j in range(bag_len):
            lo, hi = marks_of(loc_ref[f, j : j + 1, :], samples)
            u = jnp.sum(dot(rank_b, lo) * hi, axis=0, keepdims=True)
            here = own_iota == own_ref[f, j : j + 1, :]
            u_map = jnp.where(here, u, u_map)
            c_map = jnp.where(here, w_ref[f, j : j + 1, :] / wsum, c_map)
        u_ref[:, f * samples : (f + 1) * samples] = u_map
        c_ref[:, f * samples : (f + 1) * samples] = c_map


def map_call(own, loc, w, rank, groups):
    fields, _, samples = own.shape
    bags = fields * samples
    return pl.pallas_call(
        map_kernel,
        out_shape=(
            jax.ShapeDtypeStruct((groups, bags), f32),
            jax.ShapeDtypeStruct((groups, bags), f32),
        ),
        compiler_params=params(),
        cost_estimate=cost(1 << 31),
    )(own, loc, w, rank)


def half_kernel(core_ref, w_ref, b_ref, o_ref, out_ref):
    ins, cut = w_ref.shape
    out_ref[:ins, :] = w_ref[...]
    n = cut // LANES
    rows = []
    for ref in (b_ref, o_ref):
        both = ref[...].astype(f32)
        picked = jnp.where(core_ref[0] == 0, both[:n], both[n:])
        rows.append(jnp.concatenate([picked[r : r + 1] for r in range(n)], axis=1))
    rows.append(jnp.zeros((TAIL - 2, cut), f32))
    out_ref[ins:, :] = jnp.concatenate(rows, axis=0).astype(bf16)


def half_call(core, w_in, b_in, w_out):
    ins, hidden = w_in.shape
    cut = hidden // 2
    return pl.pallas_call(
        half_kernel,
        grid_spec=pltpu.PrefetchScalarGridSpec(
            num_scalar_prefetch=1,
            grid=(1,),
            in_specs=[
                pl.BlockSpec((ins, cut), lambda i, core: (0, core[0])),
                pl.BlockSpec((hidden // LANES, LANES), lambda i, core: (0, 0)),
                pl.BlockSpec((hidden // LANES, LANES), lambda i, core: (0, 0)),
            ],
            out_specs=pl.BlockSpec((ins + TAIL, cut), lambda i, core: (0, 0)),
        ),
        out_shape=jax.ShapeDtypeStruct((ins + TAIL, cut), bf16),
        compiler_params=params(("arbitrary",)),
    )(core, w_in, b_in.reshape(-1, LANES), w_out.reshape(-1, LANES))


def take_kernel(flat_ref, tb_ref, out_ref, tt_ref):
    rows, width = tb_ref.shape
    n = flat_ref.shape[1]

    @pl.when(pl.program_id(0) == 0)
    def _():
        tt_ref[...] = tb_ref[...].T.astype(bf16)

    part = 256
    for k in range(0, n, part):
        asked = flat_ref[:, k : k + part]
        marks = jnp.where(lax.broadcasted_iota(i32, (rows, part), 0) == asked, 1.0, 0.0).astype(bf16)
        out_ref[k : k + part, :] = dot(tt_ref[...], marks).T.astype(bf16)


def take_call(flat, table):
    n = flat.shape[1]
    rows, width = table.shape
    block = TAKE_BLOCK if n % TAKE_BLOCK == 0 else n
    return pl.pallas_call(
        take_kernel,
        grid=(n // block,),
        in_specs=[
            pl.BlockSpec((1, block), lambda i: (0, i)),
            pl.BlockSpec((rows, width), lambda i: (0, 0)),
        ],
        out_specs=pl.BlockSpec((block, width), lambda i: (i, 0)),
        out_shape=jax.ShapeDtypeStruct((n, width), bf16),
        scratch_shapes=[pltpu.VMEM((width, rows), bf16)],
        compiler_params=params(("arbitrary",)),
        cost_estimate=cost(2 * n * rows * width * 2),
    )(flat, table)


def build(u_ref, c_ref, cols, first, count, lo, hi):
    n = hi - lo
    iota = lax.broadcasted_iota(i32, (n, cols.stop - cols.start), 0).astype(f32) + float(lo)
    return jnp.concatenate(
        [
            jnp.where(iota == u_ref[o : o + 1, cols], c_ref[o : o + 1, cols], 0.0)
            for o in range(first, first + count)
        ],
        axis=0,
    ).astype(bf16)


def steps_of(groups, most):
    return min(most, groups)


def pool_kernel(fields, lo, hi, first, last, u_ref, c_ref, r_ref, *refs):
    per_step, bags = u_ref.shape
    samples = bags // fields
    width = r_ref.shape[1]
    x_ref, acc_ref = refs[-2:] if last else (None, refs[-1])

    @pl.when(pl.program_id(0) == 0)
    def _():
        acc_ref[...] = jnp.zeros_like(acc_ref) if first else refs[0][...]

    rt = r_ref[...].astype(f32).T.astype(bf16)
    for f in range(fields):
        cols = slice(f * samples, (f + 1) * samples)
        acc_ref[:, cols] += dot(rt, build(u_ref, c_ref, cols, 0, per_step, lo, hi))

    if last:

        @pl.when(pl.program_id(0) == pl.num_programs(0) - 1)
        def _():
            for f in range(fields):
                x_ref[:, f * width : (f + 1) * width] = acc_ref[:, f * samples : (f + 1) * samples].T.astype(bf16)


def pool_call(u, c, r, fields, lo, hi, prev, last):
    groups, bags = u.shape
    width = r.shape[1]
    per_step = steps_of(groups, POOL_STEP)
    n = hi - lo
    acc = jax.ShapeDtypeStruct((width, bags), f32)
    x = jax.ShapeDtypeStruct((bags // fields, fields * width), bf16)
    acc_spec = pl.BlockSpec((width, bags), lambda i: (0, 0))
    return pl.pallas_call(
        functools.partial(pool_kernel, fields, lo, hi, prev is None, last),
        grid=(groups // per_step,),
        in_specs=[
            pl.BlockSpec((per_step, bags), lambda i: (i, 0)),
            pl.BlockSpec((per_step, bags), lambda i: (i, 0)),
            pl.BlockSpec((per_step * n, width), lambda i: (i, 0)),
        ]
        + ([] if prev is None else [acc_spec]),
        out_specs=pl.BlockSpec(x.shape, lambda i: (0, 0)) if last else acc_spec,
        out_shape=x if last else acc,
        scratch_shapes=[pltpu.VMEM((width, bags), f32)] if last else [],
        compiler_params=params(("arbitrary",)),
        cost_estimate=cost(2 * groups * n * bags * width * 2),
    )(u, c, r, *([] if prev is None else [prev]))


def head_kernel(sides, x_ref, lab_ref, *refs):
    weights, (dt_ref, d_ref, slope_ref, acc_ref), refs = refs[: 5 * sides], refs[5 * sides : 5 * sides + 4], refs[5 * sides + 4 :]
    held, sem = refs[: 5 * sides], refs[5 * sides]
    samples, ins = x_ref.shape
    width = d_ref.shape[1]
    copies = [pltpu.make_async_copy(weights[k], held[k], sem.at[k]) for k in range(5 * sides)]
    for copy in copies:
        copy.start()
    x = x_ref[...]
    top = held[3].shape[0]
    logits = jnp.zeros((samples, 1), f32)
    blocks = [(5 * s + p,) for s in range(sides) for p in range(3)] + [(5 * s + 3, 5 * s + 4) for s in range(sides)]
    pre = None
    for k in range(len(blocks) + 1):
        done, old = pre, k - 1
        if k < len(blocks):
            block = blocks[k]
            for b in block:
                copies[b].wait()
            if len(block) == 1:
                pre = dot(x, held[block[0]][:ins, :])
            else:
                pre = dot(x[:, :top], held[block[0]][...]) + dot(x[:, top:], held[block[1]][: ins - top, :])
            last = held[block[-1]]
            at = ins if len(block) == 1 else ins - top
            pre = pre + last[at : at + 1, :].astype(f32)
        if k > 0:
            block = blocks[old]
            last = held[block[-1]]
            at = ins + 1 if len(block) == 1 else ins - top + 1
            out = last[at : at + 1, :].astype(f32)
            sig = jax.nn.sigmoid(done)
            logits = logits + jnp.sum(done * sig * out, axis=1, keepdims=True)
            slope_ref[old] = (out * (sig * (1.0 + done * (1.0 - sig)))).astype(bf16)
    logits = jnp.broadcast_to(logits, (samples, LANES)).T[:1, :]
    grad = jax.nn.sigmoid(logits) - lab_ref[...]
    for k, block in enumerate(blocks):
        slope = slope_ref[k]
        if len(block) == 1:
            part = dot(held[block[0]][:ins, :], slope, ((1,), (1,)))
            acc_ref[...] = part if k == 0 else acc_ref[...] + part
        else:
            acc_ref[:top, :] += dot(held[block[0]][...], slope, ((1,), (1,)))
            acc_ref[top:, :] += dot(held[block[1]][: ins - top, :], slope, ((1,), (1,)))
    for f in range(ins // width):
        block = acc_ref[f * width : (f + 1) * width, :] * grad
        dt_ref[f * width : (f + 1) * width, :] = block.astype(bf16)
        d_ref[f * samples : (f + 1) * samples, :] = block.T.astype(bf16)


def head_call(x, labels, weights, width):
    samples, ins = x.shape
    sides = len(weights) // 5
    cut = weights[0].shape[1]
    n = len(weights)
    vmem = pl.BlockSpec(memory_space=pltpu.VMEM)
    return pl.pallas_call(
        functools.partial(head_kernel, sides),
        in_specs=[vmem, vmem] + [pl.BlockSpec(memory_space=pl.ANY)] * n,
        out_specs=(vmem, vmem),
        out_shape=(
            jax.ShapeDtypeStruct((ins, samples), bf16),
            jax.ShapeDtypeStruct((ins // width * samples, width), bf16),
        ),
        scratch_shapes=[
            pltpu.VMEM((4 * sides, samples, cut), bf16),
            pltpu.VMEM((ins, samples), f32),
        ]
        + [pltpu.VMEM(a.shape, bf16) for a in weights]
        + [pltpu.SemaphoreType.DMA((n,))],
        compiler_params=params(),
        cost_estimate=cost(4 * samples * ins * cut * 4 * sides, 14 << 20),
    )(x, labels, *weights)


def give_kernel(fields, lo, hi, u_ref, c_ref, d_ref, g_ref):
    per_step, bags = u_ref.shape
    samples = bags // fields
    total = None
    for f in range(fields):
        cols = slice(f * samples, (f + 1) * samples)
        got = dot(build(u_ref, c_ref, cols, 0, per_step, lo, hi), d_ref[cols, :])
        total = got if total is None else total + got
    g_ref[...] = total.astype(bf16)


def give_call(u, c, d, fields, lo, hi):
    groups, bags = u.shape
    width = d.shape[1]
    per_step = steps_of(groups, GIVE_STEP)
    n = hi - lo
    return pl.pallas_call(
        functools.partial(give_kernel, fields, lo, hi),
        grid=(groups // per_step,),
        in_specs=[
            pl.BlockSpec((per_step, bags), lambda i: (i, 0)),
            pl.BlockSpec((per_step, bags), lambda i: (i, 0)),
            pl.BlockSpec((bags, width), lambda i: (0, 0)),
        ],
        out_specs=pl.BlockSpec((per_step * n, width), lambda i: (i, 0)),
        out_shape=jax.ShapeDtypeStruct((groups * n, width), bf16),
        compiler_params=params(("arbitrary",)),
        cost_estimate=cost(2 * groups * n * bags * width * 2),
    )(u, c, d)


def along_kernel(own_ref, w_ref, u_ref, dt_ref, *refs):
    r_refs, (out_ref, acc_ref) = refs[:-2], refs[-2:]
    fields, bag_len, samples = own_ref.shape
    per_step = u_ref.shape[0]
    width = r_refs[0].shape[1]
    step = pl.program_id(0)

    @pl.when(step == 0)
    def _():
        acc_ref[...] = jnp.zeros_like(acc_ref)

    for f in range(fields):
        cols = slice(f * samples, (f + 1) * samples)
        d = dt_ref[f * width : (f + 1) * width, :]
        prods = [dot(r_ref[...], d) for r_ref in r_refs]
        own = own_ref[f]
        got = acc_ref[f]
        for o in range(per_step):
            value = None
            for (lo, hi), prod in zip(CHUNKS, prods):
                n = hi - lo
                iota = lax.broadcasted_iota(i32, (n, samples), 0).astype(f32) + float(lo)
                hit = jnp.where(iota == u_ref[o : o + 1, cols], prod[o * n : (o + 1) * n, :], 0.0)
                part = jnp.sum(hit.reshape(n // 8, 8, samples), axis=0)
                value = part if value is None else value + part
            value = jnp.sum(value, axis=0, keepdims=True)
            got = jnp.where(own == step * per_step + o, value, got)
        acc_ref[f] = got

    @pl.when(step == pl.num_programs(0) - 1)
    def _():
        for f in range(fields):
            w = w_ref[f]
            wsum = jnp.sum(w, axis=0, keepdims=True)
            along = acc_ref[f]
            centre = jnp.sum(w * along, axis=0, keepdims=True) / wsum
            out_ref[f] = (along - centre) / wsum


def along_call(own, w, u, dt, rs):
    groups, bags = u.shape
    width = rs[0].shape[1]
    per_step = steps_of(groups, ALONG_STEP)
    whole3 = pl.BlockSpec(own.shape, lambda i: (0, 0, 0))
    return pl.pallas_call(
        along_kernel,
        grid=(groups // per_step,),
        in_specs=[
            whole3,
            whole3,
            pl.BlockSpec((per_step, bags), lambda i: (i, 0)),
            pl.BlockSpec(dt.shape, lambda i: (0, 0)),
        ]
        + [pl.BlockSpec((per_step * (hi - lo), width), lambda i: (i, 0)) for lo, hi in CHUNKS],
        out_specs=whole3,
        out_shape=jax.ShapeDtypeStruct(own.shape, f32),
        scratch_shapes=[pltpu.VMEM(own.shape, f32)],
        compiler_params=params(("arbitrary",)),
        cost_estimate=cost(2 * groups * UNIQ * bags * width * 2),
    )(own, w, u, dt, *rs)


def add_kernel(first, last, lo, hi, list_ref, g_ref, *refs):
    out_ref, acc_ref = refs[-2:] if last else (None, refs[-1])
    width, rows = acc_ref.shape
    per_step = list_ref.shape[0]

    @pl.when(pl.program_id(0) == 0)
    def _():
        acc_ref[...] = jnp.zeros_like(acc_ref) if first else refs[0][...]

    asked = list_ref[...].T
    columns = jnp.concatenate([asked[lo:hi, o : o + 1] for o in range(per_step)], axis=0)
    gt = g_ref[...].astype(f32).T.astype(bf16)
    part = 256
    for k in range(0, rows, part):
        iota = lax.broadcasted_iota(i32, (columns.shape[0], part), 1) + k
        marks = jnp.where(iota == columns, 1.0, 0.0).astype(bf16)
        acc_ref[:, k : k + part] += dot(gt, marks)

    if last:

        @pl.when(pl.program_id(0) == pl.num_programs(0) - 1)
        def _():
            for k in range(0, rows, part):
                out_ref[k : k + part, :] = acc_ref[:, k : k + part].T.astype(bf16)


def add_call(lists, g, rows, lo, hi, prev, last):
    groups = lists.shape[0]
    width = g.shape[1]
    per_step = steps_of(groups, ADD_STEP)
    acc = pl.BlockSpec((width, rows), lambda i: (0, 0))
    return pl.pallas_call(
        functools.partial(add_kernel, prev is None, last, lo, hi),
        grid=(groups // per_step,),
        in_specs=[
            pl.BlockSpec((per_step, LANES), lambda i: (i, 0)),
            pl.BlockSpec((per_step * (hi - lo), width), lambda i: (i, 0)),
        ]
        + ([] if prev is None else [acc]),
        out_specs=pl.BlockSpec((rows, width), lambda i: (0, 0)) if last else acc,
        out_shape=jax.ShapeDtypeStruct((rows, width), bf16) if last else jax.ShapeDtypeStruct((width, rows), f32),
        scratch_shapes=[pltpu.VMEM((width, rows), f32)] if last else [],
        compiler_params=params(("arbitrary",)),
        cost_estimate=cost(2 * g.shape[0] * rows * width * 2),
    )(lists, g, *([] if prev is None else [prev]))


def send(x, groups):
    width = x.shape[1]
    return lax.all_to_all(
        x.reshape(groups, -1, width), "owner", split_axis=0, concat_axis=0, tiled=True
    ).reshape(-1, width)


def turn(x, shift):
    dense = lax.axis_size("dense")
    return lax.ppermute(x, "dense", [(i, (i + shift) % dense) for i in range(dense)])


def swap(x):
    return lax.ppermute(x, "owner", [(i, i ^ 1) for i in range(lax.axis_size("owner"))])


def local(owners, local_rows, weights, labels, table, accum, w_in, b_in, w_out):
    fields = owners.shape[1]
    rows, width = table.shape
    groups = lax.axis_size("owner")
    dense = lax.axis_size("dense")
    own, loc, w = (a.transpose(1, 2, 0) for a in (owners, local_rows, weights))

    listed, rank = list_call(loc, groups)
    lists = lax.all_to_all(listed, "owner", split_axis=0, concat_axis=0, tiled=True)
    u, c = map_call(own, loc, w, rank, groups)

    core = (lax.axis_index("owner") % 2).astype(i32)[None]
    mine = half_call(after(core, listed), w_in, after(b_in, listed), after(w_out, listed))
    ahead, behind = turn(mine, 1), turn(mine, dense - 1)

    lists = after(lists, u)
    flat = [lists[:, lo:hi].reshape(1, groups * (hi - lo)) for lo, hi in CHUNKS]
    found = [take_call(a, table) for a in flat]
    rs = [send(x, groups) for x in found]

    near = [mine, after(ahead, found[-1]), after(behind, found[-1])]
    cut = (mine.shape[0] // 32) * 16
    far = [turn(near[1][:cut], 1), turn(near[2][cut:], dense - 1)]
    head_weights = near + far + [swap(a) for a in near + far]

    x = None
    for k, (lo, hi) in enumerate(CHUNKS):
        x = pool_call(u, c, rs[k], fields, lo, hi, x, k == len(CHUNKS) - 1)
    dt, d = head_call(x, labels.astype(f32)[None], head_weights, width)
    gs = [give_call(u, c, d, fields, lo, hi) for lo, hi in CHUNKS]
    gots = [send(g, groups) for g in gs]
    weight_grad = along_call(own, w, u, after(dt, *gs), rs)
    part = None
    for k, (lo, hi) in enumerate(CHUNKS):
        got = after(gots[k], weight_grad) if k == 0 else gots[k]
        part = add_call(lists, got, rows, lo, hi, part, k == len(CHUNKS) - 1)

    cut = rows // dense
    me = lax.axis_index("dense")
    piece = lambda k: lax.dynamic_slice_in_dim(part, lax.rem(me + k, dense) * cut, cut, axis=0)
    total = piece(0).astype(f32)
    for k in range(1, dense):
        total = total + turn(piece(k), k).astype(f32)
    total = total.astype(bf16)
    row_grad = jnp.zeros((rows, width), bf16)
    for k in range(dense):
        got = total if k == 0 else turn(total, k)
        row_grad = lax.dynamic_update_slice_in_dim(row_grad, got, lax.rem(me + dense - k, dense) * cut, axis=0)
    row_grad = row_grad.astype(f32)
    new_accum = accum + jnp.mean(row_grad * row_grad, axis=-1)
    new_table = table - step_size * row_grad / jnp.sqrt(new_accum)[:, None]
    return (new_table, new_accum, weight_grad.transpose(2, 0, 1))


def solution(mesh):
    placed = (
        P(("owner", "dense"), None, None),
        P(("owner", "dense"), None, None),
        P(("owner", "dense"), None, None),
        P(("owner", "dense")),
        P("owner", None),
        P("owner"),
        P(None, "dense"),
        P("dense"),
        P("dense"),
    )
    return jax.shard_map(
        local,
        mesh=mesh,
        in_specs=placed,
        out_specs=(P("owner", None), P("owner"), P(("owner", "dense"), None, None)),
        check_vma=False,
    )
```

```python
import functools

import jax
import jax.numpy as jnp
from jax import lax
from jax.experimental import pallas as pl
from jax.experimental.pallas import tpu as pltpu
from jax.sharding import PartitionSpec as P

step_size = 0.5
UNIQ = 104
ROWS_DEV = 2048
LANES = 128
CHUNKS = ((0, 104),)
TAIL = 16
TAKE_BLOCK, POOL_STEP, GIVE_STEP, ADD_STEP, ALONG_STEP = 3328, 32, 32, 64, 8
HEAD_CUT, HEAD_MIB, STEP_MIB = 1024, 36, 32
MIB = 1024 * 1024
f32, bf16, i32 = jnp.float32, jnp.bfloat16, jnp.int32


def dot(a, b, dims=((1,), (0,))):
    return lax.dot_general(a, b, (dims, ((), ())), preferred_element_type=f32)


def params(mib, sem=None):
    return pltpu.CompilerParams(vmem_limit_bytes=mib * MIB, dimension_semantics=sem)


def cost(flops, moved=1 << 20):
    if moved == 0:
        return pl.CostEstimate(flops=flops, bytes_accessed=1 << 10, transcendentals=0)
    return pl.CostEstimate(flops=1 << 20, bytes_accessed=1 << 10, transcendentals=0)


def after(x, *before):
    return lax.optimization_barrier((x, *before))[0]


def marks_of(row, samples):
    lo = lax.broadcasted_iota(i32, (LANES, samples), 0) == (row & (LANES - 1))
    hi = lax.broadcasted_iota(i32, (ROWS_DEV // LANES, samples), 0) == (row >> 7)
    return jnp.where(lo, 1.0, 0.0).astype(bf16), jnp.where(hi, 1.0, 0.0)


def list_kernel(loc_ref, list_ref, rank_ref):
    fields, bag_len, samples = loc_ref.shape
    his = ROWS_DEV // LANES
    count = jnp.zeros((his, LANES), f32)
    for f in range(fields):
        for j in range(bag_len):
            lo, hi = marks_of(loc_ref[f, j : j + 1, :], samples)
            count = count + dot(hi.astype(bf16), lo, ((1,), (1,)))
    present = jnp.where(count > 0.5, 1.0, 0.0)
    tri = jnp.where(
        lax.broadcasted_iota(i32, (LANES, LANES), 0) <= lax.broadcasted_iota(i32, (LANES, LANES), 1), 1.0, 0.0
    ).astype(bf16)
    upto = dot(present.astype(bf16), tri)
    below = jnp.where(
        lax.broadcasted_iota(i32, (his, his), 0) > lax.broadcasted_iota(i32, (his, his), 1), 1.0, 0.0
    ).astype(bf16)
    totals = jnp.broadcast_to(upto[:, LANES - 1 :], (his, LANES))
    rank = upto - present + dot(below, totals.astype(bf16))
    rank_ref[...] = rank
    rank_cols = jnp.where(present > 0.5, rank, -1.0).T
    lane = lax.broadcasted_iota(i32, (LANES, LANES), 1).astype(f32)
    sub = lax.broadcasted_iota(i32, (LANES, LANES), 0).astype(f32)
    listed = jnp.zeros((LANES, LANES), f32)
    for h in range(his):
        listed = listed + jnp.where(rank_cols[:, h : h + 1] == lane, sub + float(h * LANES), 0.0)
    row = jnp.sum(listed, axis=0, keepdims=True).astype(i32)
    list_ref[...] = jnp.broadcast_to(row, list_ref.shape)


def list_call(loc, groups):
    return pl.pallas_call(
        list_kernel,
        out_shape=(
            jax.ShapeDtypeStruct((groups, LANES), i32),
            jax.ShapeDtypeStruct((ROWS_DEV // LANES, LANES), f32),
        ),
        compiler_params=params(16),
        cost_estimate=cost(1 << 31),
    )(loc)


def map_kernel(own_ref, loc_ref, w_ref, rank_ref, u_ref, c_ref):
    fields, bag_len, samples = own_ref.shape
    groups = u_ref.shape[0]
    rank_b = rank_ref[...].astype(bf16)
    own_iota = lax.broadcasted_iota(i32, (groups, samples), 0)
    for f in range(fields):
        wsum = w_ref[f, 0:1, :]
        for j in range(1, bag_len):
            wsum = wsum + w_ref[f, j : j + 1, :]
        u_map = jnp.full((groups, samples), -1.0, f32)
        c_map = jnp.zeros((groups, samples), f32)
        for j in range(bag_len):
            lo, hi = marks_of(loc_ref[f, j : j + 1, :], samples)
            u = jnp.sum(dot(rank_b, lo) * hi, axis=0, keepdims=True)
            here = own_iota == own_ref[f, j : j + 1, :]
            u_map = jnp.where(here, u, u_map)
            c_map = jnp.where(here, w_ref[f, j : j + 1, :] / wsum, c_map)
        u_ref[:, f * samples : (f + 1) * samples] = u_map
        c_ref[:, f * samples : (f + 1) * samples] = c_map


def map_call(own, loc, w, rank, groups):
    fields, _, samples = own.shape
    bags = fields * samples
    return pl.pallas_call(
        map_kernel,
        out_shape=(
            jax.ShapeDtypeStruct((groups, bags), f32),
            jax.ShapeDtypeStruct((groups, bags), f32),
        ),
        compiler_params=params(16),
        cost_estimate=cost(1 << 31),
    )(own, loc, w, rank)


def take_kernel(flat_ref, tb_ref, out_ref, tt_ref):
    rows, width = tb_ref.shape
    n = flat_ref.shape[1]

    @pl.when(pl.program_id(0) == 0)
    def _():
        tt_ref[...] = tb_ref[...].T.astype(bf16)

    part = 256
    for k in range(0, n, part):
        asked = flat_ref[:, k : k + part]
        marks = jnp.where(lax.broadcasted_iota(i32, (rows, part), 0) == asked, 1.0, 0.0).astype(bf16)
        out_ref[k : k + part, :] = dot(tt_ref[...], marks).T.astype(bf16)


def take_call(flat, table):
    n = flat.shape[1]
    rows, width = table.shape
    block = TAKE_BLOCK if n % TAKE_BLOCK == 0 else n
    return pl.pallas_call(
        take_kernel,
        grid=(n // block,),
        in_specs=[
            pl.BlockSpec((1, block), lambda i: (0, i)),
            pl.BlockSpec((rows, width), lambda i: (0, 0)),
        ],
        out_specs=pl.BlockSpec((block, width), lambda i: (i, 0)),
        out_shape=jax.ShapeDtypeStruct((n, width), bf16),
        scratch_shapes=[pltpu.VMEM((width, rows), bf16)],
        compiler_params=params(STEP_MIB, ("arbitrary",)),
        cost_estimate=cost(2 * n * rows * width * 2),
    )(flat, table)


def build(u_ref, c_ref, cols, first, count, lo, hi):
    n = hi - lo
    iota = lax.broadcasted_iota(i32, (n, cols.stop - cols.start), 0).astype(f32) + float(lo)
    return jnp.concatenate(
        [
            jnp.where(iota == u_ref[o : o + 1, cols], c_ref[o : o + 1, cols], 0.0)
            for o in range(first, first + count)
        ],
        axis=0,
    ).astype(bf16)


def steps_of(groups, most):
    return min(most, groups)


def pool_kernel(fields, lo, hi, first, last, u_ref, c_ref, r_ref, *refs):
    per_step, bags = u_ref.shape
    samples = bags // fields
    width = r_ref.shape[1]
    x_ref, acc_ref = refs[-2:] if last else (None, refs[-1])

    @pl.when(pl.program_id(0) == 0)
    def _():
        acc_ref[...] = jnp.zeros_like(acc_ref) if first else refs[0][...]

    rt = r_ref[...].astype(f32).T.astype(bf16)
    for f in range(fields):
        cols = slice(f * samples, (f + 1) * samples)
        acc_ref[:, cols] += dot(rt, build(u_ref, c_ref, cols, 0, per_step, lo, hi))

    if last:

        @pl.when(pl.program_id(0) == pl.num_programs(0) - 1)
        def _():
            for f in range(fields):
                x_ref[:, f * width : (f + 1) * width] = acc_ref[:, f * samples : (f + 1) * samples].T.astype(bf16)


def pool_call(u, c, r, fields, lo, hi, prev, last):
    groups, bags = u.shape
    width = r.shape[1]
    per_step = steps_of(groups, POOL_STEP)
    n = hi - lo
    acc = jax.ShapeDtypeStruct((width, bags), f32)
    x = jax.ShapeDtypeStruct((bags // fields, fields * width), bf16)
    acc_spec = pl.BlockSpec((width, bags), lambda i: (0, 0))
    return pl.pallas_call(
        functools.partial(pool_kernel, fields, lo, hi, prev is None, last),
        grid=(groups // per_step,),
        in_specs=[
            pl.BlockSpec((per_step, bags), lambda i: (i, 0)),
            pl.BlockSpec((per_step, bags), lambda i: (i, 0)),
            pl.BlockSpec((per_step * n, width), lambda i: (i, 0)),
        ]
        + ([] if prev is None else [acc_spec]),
        out_specs=pl.BlockSpec(x.shape, lambda i: (0, 0)) if last else acc_spec,
        out_shape=x if last else acc,
        scratch_shapes=[pltpu.VMEM((width, bags), f32)] if last else [],
        compiler_params=params(STEP_MIB, ("arbitrary",)),
        cost_estimate=cost(1 << 36, 0),
    )(u, c, r, *([] if prev is None else [prev]))


def head_kernel(core_ref, x_ref, lab_ref, bw_ref, own_ref, near_ref, other_ref, far_ref, rest_ref, *refs):
    dt_ref, d_ref, slope_ref, acc_ref, held, sem = refs
    samples, ins = x_ref.shape
    width = d_ref.shape[1]
    hidden = own_ref.shape[1]
    half = far_ref.shape[0]
    core = core_ref[0]
    places = [
        (own_ref, held.at[0]),
        (near_ref, held.at[1]),
        (other_ref, held.at[2]),
        (far_ref, held.at[3, pl.ds(pl.multiple_of(core * half, half), half)]),
        (rest_ref, held.at[3, pl.ds(pl.multiple_of((1 - core) * half, half), half)]),
    ]
    copies = [pltpu.make_async_copy(a, b, sem.at[k]) for k, (a, b) in enumerate(places)]
    for copy in copies:
        copy.start()
    x = x_ref[...]
    logits = jnp.zeros((samples, 1), f32)
    cut = HEAD_CUT
    parts = [(b, slice(c, c + cut)) for b in range(4) for c in range(0, hidden, cut)]
    pre = None
    for k in range(len(parts) + 1):
        done = pre
        if k < len(parts):
            b, cols = parts[k]
            if cols.start == 0:
                copies[b].wait()
                if b == 3:
                    copies[4].wait()
            pre = dot(x, held[b, :, cols]) + bw_ref[b * TAIL : b * TAIL + 1, cols].astype(f32)
        if k > 0:
            b, cols = parts[k - 1]
            out = bw_ref[b * TAIL + 1 : b * TAIL + 2, cols].astype(f32)
            sig = jax.nn.sigmoid(done)
            logits = logits + jnp.sum(done * sig * out, axis=1, keepdims=True)
            slope_ref[b, :, cols] = (out * (sig * (1.0 + done * (1.0 - sig)))).astype(bf16)
    logits = jnp.broadcast_to(logits, (samples, LANES)).T[:1, :]
    grad = jax.nn.sigmoid(logits) - lab_ref[...]
    for b in range(4):
        part = dot(held[b], slope_ref[b], ((1,), (1,)))
        acc_ref[...] = part if b == 0 else acc_ref[...] + part
    for f in range(ins // width):
        block = acc_ref[f * width : (f + 1) * width, :] * grad
        dt_ref[f * width : (f + 1) * width, :] = block.astype(bf16)
        d_ref[f * samples : (f + 1) * samples, :] = block.T.astype(bf16)


def head_call(core, x, labels, bw, weights, width):
    samples, ins = x.shape
    hidden = weights[0].shape[1]
    vmem = pl.BlockSpec(memory_space=pltpu.VMEM)
    return pl.pallas_call(
        head_kernel,
        in_specs=[pl.BlockSpec(memory_space=pltpu.SMEM), vmem, vmem, vmem]
        + [pl.BlockSpec(memory_space=pl.ANY)] * len(weights),
        out_specs=(vmem, vmem),
        out_shape=(
            jax.ShapeDtypeStruct((ins, samples), bf16),
            jax.ShapeDtypeStruct((ins // width * samples, width), bf16),
        ),
        scratch_shapes=[
            pltpu.VMEM((4, samples, hidden), bf16),
            pltpu.VMEM((ins, samples), f32),
            pltpu.VMEM((4, ins, hidden), bf16),
            pltpu.SemaphoreType.DMA((len(weights),)),
        ],
        compiler_params=params(HEAD_MIB),
        cost_estimate=cost(4 * samples * ins * hidden * 4, 14 << 20),
    )(core, x, labels, bw, *weights)


def give_kernel(fields, lo, hi, u_ref, c_ref, d_ref, g_ref):
    per_step, bags = u_ref.shape
    samples = bags // fields
    total = None
    for f in range(fields):
        cols = slice(f * samples, (f + 1) * samples)
        got = dot(build(u_ref, c_ref, cols, 0, per_step, lo, hi), d_ref[cols, :])
        total = got if total is None else total + got
    g_ref[...] = total.astype(bf16)


def give_call(u, c, d, fields, lo, hi):
    groups, bags = u.shape
    width = d.shape[1]
    per_step = steps_of(groups, GIVE_STEP)
    n = hi - lo
    return pl.pallas_call(
        functools.partial(give_kernel, fields, lo, hi),
        grid=(groups // per_step,),
        in_specs=[
            pl.BlockSpec((per_step, bags), lambda i: (i, 0)),
            pl.BlockSpec((per_step, bags), lambda i: (i, 0)),
            pl.BlockSpec((bags, width), lambda i: (0, 0)),
        ],
        out_specs=pl.BlockSpec((per_step * n, width), lambda i: (i, 0)),
        out_shape=jax.ShapeDtypeStruct((groups * n, width), bf16),
        compiler_params=params(STEP_MIB, ("arbitrary",)),
        cost_estimate=cost(2 * groups * n * bags * width * 2),
    )(u, c, d)


def along_kernel(own_ref, w_ref, u_ref, dt_ref, *refs):
    r_refs, (out_ref, acc_ref) = refs[:-2], refs[-2:]
    fields, bag_len, samples = own_ref.shape
    per_step = u_ref.shape[0]
    width = r_refs[0].shape[1]
    step = pl.program_id(0)

    @pl.when(step == 0)
    def _():
        acc_ref[...] = jnp.zeros_like(acc_ref)

    for f in range(fields):
        cols = slice(f * samples, (f + 1) * samples)
        d = dt_ref[f * width : (f + 1) * width, :]
        prods = [dot(r_ref[...], d) for r_ref in r_refs]
        own = own_ref[f]
        got = acc_ref[f]
        for o in range(per_step):
            value = None
            for (lo, hi), prod in zip(CHUNKS, prods):
                n = hi - lo
                iota = lax.broadcasted_iota(i32, (n, samples), 0).astype(f32) + float(lo)
                hit = jnp.where(iota == u_ref[o : o + 1, cols], prod[o * n : (o + 1) * n, :], 0.0)
                part = jnp.sum(hit.reshape(n // 8, 8, samples), axis=0)
                value = part if value is None else value + part
            value = jnp.sum(value, axis=0, keepdims=True)
            got = jnp.where(own == step * per_step + o, value, got)
        acc_ref[f] = got

    @pl.when(step == pl.num_programs(0) - 1)
    def _():
        for f in range(fields):
            w = w_ref[f]
            wsum = jnp.sum(w, axis=0, keepdims=True)
            along = acc_ref[f]
            centre = jnp.sum(w * along, axis=0, keepdims=True) / wsum
            out_ref[f] = (along - centre) / wsum


def along_call(own, w, u, dt, rs):
    groups, bags = u.shape
    width = rs[0].shape[1]
    per_step = steps_of(groups, ALONG_STEP)
    whole3 = pl.BlockSpec(own.shape, lambda i: (0, 0, 0))
    return pl.pallas_call(
        along_kernel,
        grid=(groups // per_step,),
        in_specs=[
            whole3,
            whole3,
            pl.BlockSpec((per_step, bags), lambda i: (i, 0)),
            pl.BlockSpec(dt.shape, lambda i: (0, 0)),
        ]
        + [pl.BlockSpec((per_step * (hi - lo), width), lambda i: (i, 0)) for lo, hi in CHUNKS],
        out_specs=whole3,
        out_shape=jax.ShapeDtypeStruct(own.shape, f32),
        scratch_shapes=[pltpu.VMEM(own.shape, f32)],
        compiler_params=params(STEP_MIB, ("arbitrary",)),
        cost_estimate=cost(2 * groups * UNIQ * bags * width * 2),
    )(own, w, u, dt, *rs)


def add_kernel(first, last, lo, hi, list_ref, g_ref, *refs):
    out_ref, acc_ref = refs[-2:] if last else (None, refs[-1])
    width, rows = acc_ref.shape
    per_step = list_ref.shape[0]

    @pl.when(pl.program_id(0) == 0)
    def _():
        acc_ref[...] = jnp.zeros_like(acc_ref) if first else refs[0][...]

    asked = list_ref[...].T
    columns = jnp.concatenate([asked[lo:hi, o : o + 1] for o in range(per_step)], axis=0)
    gt = g_ref[...].astype(f32).T.astype(bf16)
    part = 256
    for k in range(0, rows, part):
        iota = lax.broadcasted_iota(i32, (columns.shape[0], part), 1) + k
        marks = jnp.where(iota == columns, 1.0, 0.0).astype(bf16)
        acc_ref[:, k : k + part] += dot(gt, marks)

    if last:

        @pl.when(pl.program_id(0) == pl.num_programs(0) - 1)
        def _():
            for k in range(0, rows, part):
                out_ref[k : k + part, :] = acc_ref[:, k : k + part].T.astype(bf16)


def add_call(lists, g, rows, lo, hi, prev, last):
    groups = lists.shape[0]
    width = g.shape[1]
    per_step = steps_of(groups, ADD_STEP)
    acc = pl.BlockSpec((width, rows), lambda i: (0, 0))
    return pl.pallas_call(
        functools.partial(add_kernel, prev is None, last, lo, hi),
        grid=(groups // per_step,),
        in_specs=[
            pl.BlockSpec((per_step, LANES), lambda i: (i, 0)),
            pl.BlockSpec((per_step * (hi - lo), width), lambda i: (i, 0)),
        ]
        + ([] if prev is None else [acc]),
        out_specs=pl.BlockSpec((rows, width), lambda i: (0, 0)) if last else acc,
        out_shape=jax.ShapeDtypeStruct((rows, width), bf16) if last else jax.ShapeDtypeStruct((width, rows), f32),
        scratch_shapes=[pltpu.VMEM((width, rows), f32)] if last else [],
        compiler_params=params(STEP_MIB, ("arbitrary",)),
        cost_estimate=cost(2 * g.shape[0] * rows * width * 2),
    )(lists, g, *([] if prev is None else [prev]))


def send(x, groups):
    width = x.shape[1]
    return lax.all_to_all(
        x.reshape(groups, -1, width), "owner", split_axis=0, concat_axis=0, tiled=True
    ).reshape(-1, width)


def turn(x, shift):
    dense = lax.axis_size("dense")
    return lax.ppermute(x, "dense", [(i, (i + shift) % dense) for i in range(dense)])


def hop(x):
    groups, dense = lax.axis_size("owner"), lax.axis_size("dense")
    pairs = [(o * dense + q, o * dense + (q + 1 - 2 * (o % 2)) % dense) for o in range(groups) for q in range(dense)]
    return lax.ppermute(x, ("owner", "dense"), pairs)


def swap(x):
    return lax.ppermute(x, "owner", [(i, i ^ 1) for i in range(lax.axis_size("owner"))])


def local(owners, local_rows, weights, labels, table, accum, w_in, b_in, w_out):
    fields = owners.shape[1]
    rows, width = table.shape
    groups = lax.axis_size("owner")
    dense = lax.axis_size("dense")
    own, loc, w = (a.transpose(1, 2, 0) for a in (owners, local_rows, weights))

    near = hop(w_in)
    listed, rank = list_call(loc, groups)
    lists = lax.all_to_all(listed, "owner", split_axis=0, concat_axis=0, tiled=True)
    flat = [lists[:, lo:hi].reshape(1, groups * (hi - lo)) for lo, hi in CHUNKS]
    found = [take_call(a, table) for a in flat]
    rs = [send(x, groups) for x in found]
    u, c = map_call(own, loc, w, after(rank, *found), groups)

    core = (lax.axis_index("owner") % 2).astype(i32)
    half = w_in.shape[0] // 2
    near = after(near, u)
    far = hop(lax.dynamic_slice_in_dim(near, core * half, half, axis=0))
    bw = jnp.concatenate([b_in[None], w_out[None], jnp.zeros((TAIL - 2, w_in.shape[1]), bf16)], axis=0)
    bw = after(bw, u)
    bw_near = hop(bw)
    bw = jnp.concatenate([bw, bw_near, swap(bw_near), hop(bw_near)], axis=0)
    head_weights = [w_in, near, swap(near), far, swap(far)]

    x = None
    for k, (lo, hi) in enumerate(CHUNKS):
        x = pool_call(u, c, after(rs[k], far), fields, lo, hi, x, k == len(CHUNKS) - 1)
    dt, d = head_call(core[None], x, labels.astype(f32)[None], bw, head_weights, width)
    gs = [give_call(u, c, d, fields, lo, hi) for lo, hi in CHUNKS]
    gots = [send(g, groups) for g in gs]
    weight_grad = along_call(own, w, u, after(dt, *gs), rs)
    part = None
    for k, (lo, hi) in enumerate(CHUNKS):
        got = after(gots[k], weight_grad) if k == 0 else gots[k]
        part = add_call(lists, got, rows, lo, hi, part, k == len(CHUNKS) - 1)

    cut = rows // dense
    me = lax.axis_index("dense")
    piece = lambda k: lax.dynamic_slice_in_dim(part, lax.rem(me + k, dense) * cut, cut, axis=0)
    total = piece(0).astype(f32)
    for k in range(1, dense):
        total = total + turn(piece(k), k).astype(f32)
    total = total.astype(bf16)
    row_grad = jnp.zeros((rows, width), bf16)
    for k in range(dense):
        got = total if k == 0 else turn(total, k)
        row_grad = lax.dynamic_update_slice_in_dim(row_grad, got, lax.rem(me + dense - k, dense) * cut, axis=0)
    row_grad = row_grad.astype(f32)
    new_accum = accum + jnp.mean(row_grad * row_grad, axis=-1)
    new_table = table - step_size * row_grad / jnp.sqrt(new_accum)[:, None]
    return (new_table, new_accum, weight_grad.transpose(2, 0, 1))


def solution(mesh):
    placed = (
        P(("owner", "dense"), None, None),
        P(("owner", "dense"), None, None),
        P(("owner", "dense"), None, None),
        P(("owner", "dense")),
        P("owner", None),
        P("owner"),
        P(None, "dense"),
        P("dense"),
        P("dense"),
    )
    return jax.shard_map(
        local,
        mesh=mesh,
        in_specs=placed,
        out_specs=(P("owner", None), P("owner"), P(("owner", "dense"), None, None)),
        check_vma=False,
    )
```

```python
import functools

import jax
import jax.numpy as jnp
from jax import lax
from jax.experimental import pallas as pl
from jax.experimental.pallas import tpu as pltpu
from jax.sharding import PartitionSpec as P

step_size = 0.5
UNIQ = 104
ROWS_DEV = 2048
LANES = 128
CHUNKS = ((0, 104),)
TAIL = 16
TAKE_BLOCK, POOL_STEP, GIVE_STEP, ADD_STEP, ALONG_STEP = 3328, 32, 32, 64, 8
HEAD_CUT, HEAD_MIB, STEP_MIB = 1024, 36, 32
MIB = 1024 * 1024
f32, bf16, i32 = jnp.float32, jnp.bfloat16, jnp.int32


def dot(a, b, dims=((1,), (0,))):
    return lax.dot_general(a, b, (dims, ((), ())), preferred_element_type=f32)


def params(mib, sem=None):
    return pltpu.CompilerParams(vmem_limit_bytes=mib * MIB, dimension_semantics=sem)


def cost(flops, moved=1 << 20):
    if moved == 0:
        return pl.CostEstimate(flops=flops, bytes_accessed=1 << 10, transcendentals=0)
    return pl.CostEstimate(flops=1 << 20, bytes_accessed=1 << 10, transcendentals=0)


def after(x, *before):
    return lax.optimization_barrier((x, *before))[0]


def marks_of(row, samples):
    lo = lax.broadcasted_iota(i32, (LANES, samples), 0) == (row & (LANES - 1))
    hi = lax.broadcasted_iota(i32, (ROWS_DEV // LANES, samples), 0) == (row >> 7)
    return jnp.where(lo, 1.0, 0.0).astype(bf16), jnp.where(hi, 1.0, 0.0)


def list_kernel(loc_ref, list_ref, rank_ref):
    fields, bag_len, samples = loc_ref.shape
    his = ROWS_DEV // LANES
    count = jnp.zeros((his, LANES), f32)
    for f in range(fields):
        for j in range(bag_len):
            lo, hi = marks_of(loc_ref[f, j : j + 1, :], samples)
            count = count + dot(hi.astype(bf16), lo, ((1,), (1,)))
    present = jnp.where(count > 0.5, 1.0, 0.0)
    tri = jnp.where(
        lax.broadcasted_iota(i32, (LANES, LANES), 0) <= lax.broadcasted_iota(i32, (LANES, LANES), 1), 1.0, 0.0
    ).astype(bf16)
    upto = dot(present.astype(bf16), tri)
    below = jnp.where(
        lax.broadcasted_iota(i32, (his, his), 0) > lax.broadcasted_iota(i32, (his, his), 1), 1.0, 0.0
    ).astype(bf16)
    totals = jnp.broadcast_to(upto[:, LANES - 1 :], (his, LANES))
    rank = upto - present + dot(below, totals.astype(bf16))
    rank_ref[...] = rank
    rank_cols = jnp.where(present > 0.5, rank, -1.0).T
    lane = lax.broadcasted_iota(i32, (LANES, LANES), 1).astype(f32)
    sub = lax.broadcasted_iota(i32, (LANES, LANES), 0).astype(f32)
    listed = jnp.zeros((LANES, LANES), f32)
    for h in range(his):
        listed = listed + jnp.where(rank_cols[:, h : h + 1] == lane, sub + float(h * LANES), 0.0)
    row = jnp.sum(listed, axis=0, keepdims=True).astype(i32)
    list_ref[...] = jnp.broadcast_to(row, list_ref.shape)


def list_call(loc, groups):
    return pl.pallas_call(
        list_kernel,
        out_shape=(
            jax.ShapeDtypeStruct((groups, LANES), i32),
            jax.ShapeDtypeStruct((ROWS_DEV // LANES, LANES), f32),
        ),
        compiler_params=params(16),
        cost_estimate=cost(1 << 31),
    )(loc)


def map_kernel(own_ref, loc_ref, w_ref, rank_ref, u_ref, c_ref):
    fields, bag_len, samples = own_ref.shape
    groups = u_ref.shape[0]
    rank_b = rank_ref[...].astype(bf16)
    own_iota = lax.broadcasted_iota(i32, (groups, samples), 0)
    for f in range(fields):
        wsum = w_ref[f, 0:1, :]
        for j in range(1, bag_len):
            wsum = wsum + w_ref[f, j : j + 1, :]
        u_map = jnp.full((groups, samples), -1.0, f32)
        c_map = jnp.zeros((groups, samples), f32)
        for j in range(bag_len):
            lo, hi = marks_of(loc_ref[f, j : j + 1, :], samples)
            u = jnp.sum(dot(rank_b, lo) * hi, axis=0, keepdims=True)
            here = own_iota == own_ref[f, j : j + 1, :]
            u_map = jnp.where(here, u, u_map)
            c_map = jnp.where(here, w_ref[f, j : j + 1, :] / wsum, c_map)
        u_ref[:, f * samples : (f + 1) * samples] = u_map
        c_ref[:, f * samples : (f + 1) * samples] = c_map


def map_call(own, loc, w, rank, groups):
    fields, _, samples = own.shape
    bags = fields * samples
    return pl.pallas_call(
        map_kernel,
        out_shape=(
            jax.ShapeDtypeStruct((groups, bags), f32),
            jax.ShapeDtypeStruct((groups, bags), f32),
        ),
        compiler_params=params(16),
        cost_estimate=cost(1 << 31),
    )(own, loc, w, rank)


def take_kernel(flat_ref, tb_ref, out_ref, tt_ref):
    rows, width = tb_ref.shape
    n = flat_ref.shape[1]

    @pl.when(pl.program_id(0) == 0)
    def _():
        tt_ref[...] = tb_ref[...].T.astype(bf16)

    part = 256
    for k in range(0, n, part):
        asked = flat_ref[:, k : k + part]
        marks = jnp.where(lax.broadcasted_iota(i32, (rows, part), 0) == asked, 1.0, 0.0).astype(bf16)
        out_ref[k : k + part, :] = dot(tt_ref[...], marks).T.astype(bf16)


def take_call(flat, table):
    n = flat.shape[1]
    rows, width = table.shape
    block = TAKE_BLOCK if n % TAKE_BLOCK == 0 else n
    return pl.pallas_call(
        take_kernel,
        grid=(n // block,),
        in_specs=[
            pl.BlockSpec((1, block), lambda i: (0, i)),
            pl.BlockSpec((rows, width), lambda i: (0, 0)),
        ],
        out_specs=pl.BlockSpec((block, width), lambda i: (i, 0)),
        out_shape=jax.ShapeDtypeStruct((n, width), bf16),
        scratch_shapes=[pltpu.VMEM((width, rows), bf16)],
        compiler_params=params(STEP_MIB, ("arbitrary",)),
        cost_estimate=cost(2 * n * rows * width * 2),
    )(flat, table)


def build(u_ref, c_ref, cols, first, count, lo, hi):
    n = hi - lo
    iota = lax.broadcasted_iota(i32, (n, cols.stop - cols.start), 0).astype(f32) + float(lo)
    return jnp.concatenate(
        [
            jnp.where(iota == u_ref[o : o + 1, cols], c_ref[o : o + 1, cols], 0.0)
            for o in range(first, first + count)
        ],
        axis=0,
    ).astype(bf16)


def steps_of(groups, most):
    return min(most, groups)


def pool_kernel(fields, lo, hi, first, last, u_ref, c_ref, r_ref, *refs):
    per_step, bags = u_ref.shape
    samples = bags // fields
    width = r_ref.shape[1]
    x_ref, acc_ref = refs[-2:] if last else (None, refs[-1])

    @pl.when(pl.program_id(0) == 0)
    def _():
        acc_ref[...] = jnp.zeros_like(acc_ref) if first else refs[0][...]

    rt = r_ref[...].astype(f32).T.astype(bf16)
    for f in range(fields):
        cols = slice(f * samples, (f + 1) * samples)
        acc_ref[:, cols] += dot(rt, build(u_ref, c_ref, cols, 0, per_step, lo, hi))

    if last:

        @pl.when(pl.program_id(0) == pl.num_programs(0) - 1)
        def _():
            for f in range(fields):
                x_ref[:, f * width : (f + 1) * width] = acc_ref[:, f * samples : (f + 1) * samples].T.astype(bf16)


def pool_call(u, c, r, fields, lo, hi, prev, last):
    groups, bags = u.shape
    width = r.shape[1]
    per_step = steps_of(groups, POOL_STEP)
    n = hi - lo
    acc = jax.ShapeDtypeStruct((width, bags), f32)
    x = jax.ShapeDtypeStruct((bags // fields, fields * width), bf16)
    acc_spec = pl.BlockSpec((width, bags), lambda i: (0, 0))
    return pl.pallas_call(
        functools.partial(pool_kernel, fields, lo, hi, prev is None, last),
        grid=(groups // per_step,),
        in_specs=[
            pl.BlockSpec((per_step, bags), lambda i: (i, 0)),
            pl.BlockSpec((per_step, bags), lambda i: (i, 0)),
            pl.BlockSpec((per_step * n, width), lambda i: (i, 0)),
        ]
        + ([] if prev is None else [acc_spec]),
        out_specs=pl.BlockSpec(x.shape, lambda i: (0, 0)) if last else acc_spec,
        out_shape=x if last else acc,
        scratch_shapes=[pltpu.VMEM((width, bags), f32)] if last else [],
        compiler_params=params(56, ("arbitrary",)),
        cost_estimate=cost(1<<34, 0),
    )(u, c, r, *([] if prev is None else [prev]))


def head_kernel(core_ref, x_ref, lab_ref, bw_ref, own_ref, near_ref, other_ref, far_ref, rest_ref, *refs):
    dt_ref, d_ref, slope_ref, acc_ref, held, sem = refs
    samples, ins = x_ref.shape
    width = d_ref.shape[1]
    hidden = own_ref.shape[1]
    half = far_ref.shape[0]
    core = core_ref[0]
    places = [
        (own_ref, held.at[0]),
        (near_ref, held.at[1]),
        (other_ref, held.at[2]),
        (far_ref, held.at[3, pl.ds(pl.multiple_of(core * half, half), half)]),
        (rest_ref, held.at[3, pl.ds(pl.multiple_of((1 - core) * half, half), half)]),
    ]
    copies = [pltpu.make_async_copy(a, b, sem.at[k]) for k, (a, b) in enumerate(places)]
    for copy in copies:
        copy.start()
    x = x_ref[...]
    logits = jnp.zeros((samples, 1), f32)
    cut = HEAD_CUT
    parts = [(b, slice(c, c + cut)) for b in range(4) for c in range(0, hidden, cut)]
    pre = None
    for k in range(len(parts) + 1):
        done = pre
        if k < len(parts):
            b, cols = parts[k]
            if cols.start == 0:
                copies[b].wait()
                if b == 3:
                    copies[4].wait()
            pre = dot(x, held[b, :, cols]) + bw_ref[b * TAIL : b * TAIL + 1, cols].astype(f32)
        if k > 0:
            b, cols = parts[k - 1]
            out = bw_ref[b * TAIL + 1 : b * TAIL + 2, cols].astype(f32)
            sig = jax.nn.sigmoid(done)
            logits = logits + jnp.sum(done * sig * out, axis=1, keepdims=True)
            slope_ref[b, :, cols] = (out * (sig * (1.0 + done * (1.0 - sig)))).astype(bf16)
    logits = jnp.broadcast_to(logits, (samples, LANES)).T[:1, :]
    grad = jax.nn.sigmoid(logits) - lab_ref[...]
    for b in range(4):
        part = dot(held[b], slope_ref[b], ((1,), (1,)))
        acc_ref[...] = part if b == 0 else acc_ref[...] + part
    for f in range(ins // width):
        block = acc_ref[f * width : (f + 1) * width, :] * grad
        dt_ref[f * width : (f + 1) * width, :] = block.astype(bf16)
        d_ref[f * samples : (f + 1) * samples, :] = block.T.astype(bf16)


def head_call(core, x, labels, bw, weights, width):
    samples, ins = x.shape
    hidden = weights[0].shape[1]
    vmem = pl.BlockSpec(memory_space=pltpu.VMEM)
    return pl.pallas_call(
        head_kernel,
        in_specs=[pl.BlockSpec(memory_space=pltpu.SMEM), vmem, vmem, vmem]
        + [pl.BlockSpec(memory_space=pl.ANY)] * len(weights),
        out_specs=(vmem, vmem),
        out_shape=(
            jax.ShapeDtypeStruct((ins, samples), bf16),
            jax.ShapeDtypeStruct((ins // width * samples, width), bf16),
        ),
        scratch_shapes=[
            pltpu.VMEM((4, samples, hidden), bf16),
            pltpu.VMEM((ins, samples), f32),
            pltpu.VMEM((4, ins, hidden), bf16),
            pltpu.SemaphoreType.DMA((len(weights),)),
        ],
        compiler_params=params(HEAD_MIB),
        cost_estimate=cost(4 * samples * ins * hidden * 4, 14 << 20),
    )(core, x, labels, bw, *weights)


def give_kernel(fields, lo, hi, u_ref, c_ref, d_ref, g_ref):
    per_step, bags = u_ref.shape
    samples = bags // fields
    total = None
    for f in range(fields):
        cols = slice(f * samples, (f + 1) * samples)
        got = dot(build(u_ref, c_ref, cols, 0, per_step, lo, hi), d_ref[cols, :])
        total = got if total is None else total + got
    g_ref[...] = total.astype(bf16)


def give_call(u, c, d, fields, lo, hi):
    groups, bags = u.shape
    width = d.shape[1]
    per_step = steps_of(groups, GIVE_STEP)
    n = hi - lo
    return pl.pallas_call(
        functools.partial(give_kernel, fields, lo, hi),
        grid=(groups // per_step,),
        in_specs=[
            pl.BlockSpec((per_step, bags), lambda i: (i, 0)),
            pl.BlockSpec((per_step, bags), lambda i: (i, 0)),
            pl.BlockSpec((bags, width), lambda i: (0, 0)),
        ],
        out_specs=pl.BlockSpec((per_step * n, width), lambda i: (i, 0)),
        out_shape=jax.ShapeDtypeStruct((groups * n, width), bf16),
        compiler_params=params(STEP_MIB, ("arbitrary",)),
        cost_estimate=cost(2 * groups * n * bags * width * 2),
    )(u, c, d)


def along_kernel(own_ref, w_ref, u_ref, dt_ref, *refs):
    r_refs, (out_ref, acc_ref) = refs[:-2], refs[-2:]
    fields, bag_len, samples = own_ref.shape
    per_step = u_ref.shape[0]
    width = r_refs[0].shape[1]
    step = pl.program_id(0)

    @pl.when(step == 0)
    def _():
        acc_ref[...] = jnp.zeros_like(acc_ref)

    for f in range(fields):
        cols = slice(f * samples, (f + 1) * samples)
        d = dt_ref[f * width : (f + 1) * width, :]
        prods = [dot(r_ref[...], d) for r_ref in r_refs]
        own = own_ref[f]
        got = acc_ref[f]
        for o in range(per_step):
            value = None
            for (lo, hi), prod in zip(CHUNKS, prods):
                n = hi - lo
                iota = lax.broadcasted_iota(i32, (n, samples), 0).astype(f32) + float(lo)
                hit = jnp.where(iota == u_ref[o : o + 1, cols], prod[o * n : (o + 1) * n, :], 0.0)
                part = jnp.sum(hit.reshape(n // 8, 8, samples), axis=0)
                value = part if value is None else value + part
            value = jnp.sum(value, axis=0, keepdims=True)
            got = jnp.where(own == step * per_step + o, value, got)
        acc_ref[f] = got

    @pl.when(step == pl.num_programs(0) - 1)
    def _():
        for f in range(fields):
            w = w_ref[f]
            wsum = jnp.sum(w, axis=0, keepdims=True)
            along = acc_ref[f]
            centre = jnp.sum(w * along, axis=0, keepdims=True) / wsum
            out_ref[f] = (along - centre) / wsum


def along_call(own, w, u, dt, rs):
    groups, bags = u.shape
    width = rs[0].shape[1]
    per_step = steps_of(groups, ALONG_STEP)
    whole3 = pl.BlockSpec(own.shape, lambda i: (0, 0, 0))
    return pl.pallas_call(
        along_kernel,
        grid=(groups // per_step,),
        in_specs=[
            whole3,
            whole3,
            pl.BlockSpec((per_step, bags), lambda i: (i, 0)),
            pl.BlockSpec(dt.shape, lambda i: (0, 0)),
        ]
        + [pl.BlockSpec((per_step * (hi - lo), width), lambda i: (i, 0)) for lo, hi in CHUNKS],
        out_specs=whole3,
        out_shape=jax.ShapeDtypeStruct(own.shape, f32),
        scratch_shapes=[pltpu.VMEM(own.shape, f32)],
        compiler_params=params(STEP_MIB, ("arbitrary",)),
        cost_estimate=cost(2 * groups * UNIQ * bags * width * 2),
    )(own, w, u, dt, *rs)


def add_kernel(first, last, lo, hi, list_ref, g_ref, *refs):
    out_ref, acc_ref = refs[-2:] if last else (None, refs[-1])
    width, rows = acc_ref.shape
    per_step = list_ref.shape[0]

    @pl.when(pl.program_id(0) == 0)
    def _():
        acc_ref[...] = jnp.zeros_like(acc_ref) if first else refs[0][...]

    asked = list_ref[...].T
    columns = jnp.concatenate([asked[lo:hi, o : o + 1] for o in range(per_step)], axis=0)
    gt = g_ref[...].astype(f32).T.astype(bf16)
    part = 256
    for k in range(0, rows, part):
        iota = lax.broadcasted_iota(i32, (columns.shape[0], part), 1) + k
        marks = jnp.where(iota == columns, 1.0, 0.0).astype(bf16)
        acc_ref[:, k : k + part] += dot(gt, marks)

    if last:

        @pl.when(pl.program_id(0) == pl.num_programs(0) - 1)
        def _():
            for k in range(0, rows, part):
                out_ref[k : k + part, :] = acc_ref[:, k : k + part].T.astype(bf16)


def add_call(lists, g, rows, lo, hi, prev, last):
    groups = lists.shape[0]
    width = g.shape[1]
    per_step = steps_of(groups, ADD_STEP)
    acc = pl.BlockSpec((width, rows), lambda i: (0, 0))
    return pl.pallas_call(
        functools.partial(add_kernel, prev is None, last, lo, hi),
        grid=(groups // per_step,),
        in_specs=[
            pl.BlockSpec((per_step, LANES), lambda i: (i, 0)),
            pl.BlockSpec((per_step * (hi - lo), width), lambda i: (i, 0)),
        ]
        + ([] if prev is None else [acc]),
        out_specs=pl.BlockSpec((rows, width), lambda i: (0, 0)) if last else acc,
        out_shape=jax.ShapeDtypeStruct((rows, width), bf16) if last else jax.ShapeDtypeStruct((width, rows), f32),
        scratch_shapes=[pltpu.VMEM((width, rows), f32)] if last else [],
        compiler_params=params(STEP_MIB, ("arbitrary",)),
        cost_estimate=cost(2 * g.shape[0] * rows * width * 2),
    )(lists, g, *([] if prev is None else [prev]))


def send(x, groups):
    width = x.shape[1]
    return lax.all_to_all(
        x.reshape(groups, -1, width), "owner", split_axis=0, concat_axis=0, tiled=True
    ).reshape(-1, width)


def turn(x, shift):
    dense = lax.axis_size("dense")
    return lax.ppermute(x, "dense", [(i, (i + shift) % dense) for i in range(dense)])


def hop(x):
    groups, dense = lax.axis_size("owner"), lax.axis_size("dense")
    pairs = [(o * dense + q, o * dense + (q + 1 - 2 * (o % 2)) % dense) for o in range(groups) for q in range(dense)]
    return lax.ppermute(x, ("owner", "dense"), pairs)


def swap(x):
    return lax.ppermute(x, "owner", [(i, i ^ 1) for i in range(lax.axis_size("owner"))])


def local(owners, local_rows, weights, labels, table, accum, w_in, b_in, w_out):
    fields = owners.shape[1]
    rows, width = table.shape
    groups = lax.axis_size("owner")
    dense = lax.axis_size("dense")
    own, loc, w = (a.transpose(1, 2, 0) for a in (owners, local_rows, weights))

    near = hop(w_in)
    listed, rank = list_call(loc, groups)
    lists = lax.all_to_all(listed, "owner", split_axis=0, concat_axis=0, tiled=True)
    flat = [lists[:, lo:hi].reshape(1, groups * (hi - lo)) for lo, hi in CHUNKS]
    found = [take_call(a, table) for a in flat]
    rs = [send(x, groups) for x in found]
    u, c = map_call(own, loc, w, after(rank, *found), groups)

    core = (lax.axis_index("owner") % 2).astype(i32)
    half = w_in.shape[0] // 2
    near = after(near, u)
    far = hop(lax.dynamic_slice_in_dim(near, core * half, half, axis=0))
    bw = jnp.concatenate([b_in[None], w_out[None], jnp.zeros((TAIL - 2, w_in.shape[1]), bf16)], axis=0)
    bw = after(bw, u)
    bw_near = hop(bw)
    bw = jnp.concatenate([bw, bw_near, swap(bw_near), hop(bw_near)], axis=0)
    other = swap(near)
    rest = swap(far)
    head_weights = [w_in, near, other, far, rest]

    x = None
    for k, (lo, hi) in enumerate(CHUNKS):
        x = pool_call(u, c, after(rs[k], far), fields, lo, hi, x, k == len(CHUNKS) - 1)
    dt, d = head_call(core[None], x, labels.astype(f32)[None], bw, head_weights, width)
    gs = [give_call(u, c, d, fields, lo, hi) for lo, hi in CHUNKS]
    gots = [send(g, groups) for g in gs]
    weight_grad = along_call(own, w, u, after(dt, *gs), rs)
    part = None
    for k, (lo, hi) in enumerate(CHUNKS):
        got = after(gots[k], weight_grad) if k == 0 else gots[k]
        part = add_call(lists, got, rows, lo, hi, part, k == len(CHUNKS) - 1)

    cut = rows // dense
    me = lax.axis_index("dense")
    piece = lambda k: lax.dynamic_slice_in_dim(part, lax.rem(me + k, dense) * cut, cut, axis=0)
    total = piece(0).astype(f32)
    for k in range(1, dense):
        total = total + turn(piece(k), k).astype(f32)
    total = total.astype(bf16)
    row_grad = jnp.zeros((rows, width), bf16)
    for k in range(dense):
        got = total if k == 0 else turn(total, k)
        row_grad = lax.dynamic_update_slice_in_dim(row_grad, got, lax.rem(me + dense - k, dense) * cut, axis=0)
    row_grad = row_grad.astype(f32)
    new_accum = accum + jnp.mean(row_grad * row_grad, axis=-1)
    new_table = table - step_size * row_grad / jnp.sqrt(new_accum)[:, None]
    return (new_table, new_accum, weight_grad.transpose(2, 0, 1))


def solution(mesh):
    placed = (
        P(("owner", "dense"), None, None),
        P(("owner", "dense"), None, None),
        P(("owner", "dense"), None, None),
        P(("owner", "dense")),
        P("owner", None),
        P("owner"),
        P(None, "dense"),
        P("dense"),
        P("dense"),
    )
    return jax.shard_map(
        local,
        mesh=mesh,
        in_specs=placed,
        out_specs=(P("owner", None), P("owner"), P(("owner", "dense"), None, None)),
        check_vma=False,
    )
```

```python
import functools

import jax
import jax.numpy as jnp
from jax import lax
from jax.experimental import pallas as pl
from jax.experimental.pallas import tpu as pltpu
from jax.sharding import PartitionSpec as P

step_size = 0.5
UNIQ = 104
ROWS_DEV = 2048
LANES = 128
CHUNKS = ((0, 104),)
TAIL = 16
TAKE_BLOCK, POOL_STEP, GIVE_STEP, ADD_STEP, ALONG_STEP = 3328, 32, 16, 32, 8
HEAD_CUT, HEAD_MIB, STEP_MIB = 1024, 36, 32
MIB = 1024 * 1024
f32, bf16, i32 = jnp.float32, jnp.bfloat16, jnp.int32


def dot(a, b, dims=((1,), (0,))):
    return lax.dot_general(a, b, (dims, ((), ())), preferred_element_type=f32)


def params(mib, sem=None):
    return pltpu.CompilerParams(vmem_limit_bytes=mib * MIB, dimension_semantics=sem)


def cost(flops, moved=1 << 20):
    if moved == 0:
        return pl.CostEstimate(flops=flops, bytes_accessed=1 << 10, transcendentals=0)
    return pl.CostEstimate(flops=1 << 20, bytes_accessed=1 << 10, transcendentals=0)


def after(x, *before):
    return lax.optimization_barrier((x, *before))[0]


def marks_of(row, samples):
    lo = lax.broadcasted_iota(i32, (LANES, samples), 0) == (row & (LANES - 1))
    hi = lax.broadcasted_iota(i32, (ROWS_DEV // LANES, samples), 0) == (row >> 7)
    return jnp.where(lo, 1.0, 0.0).astype(bf16), jnp.where(hi, 1.0, 0.0)


def list_kernel(loc_ref, list_ref, rank_ref):
    fields, bag_len, samples = loc_ref.shape
    his = ROWS_DEV // LANES
    count = jnp.zeros((his, LANES), f32)
    for f in range(fields):
        for j in range(bag_len):
            lo, hi = marks_of(loc_ref[f, j : j + 1, :], samples)
            count = count + dot(hi.astype(bf16), lo, ((1,), (1,)))
    present = jnp.where(count > 0.5, 1.0, 0.0)
    tri = jnp.where(
        lax.broadcasted_iota(i32, (LANES, LANES), 0) <= lax.broadcasted_iota(i32, (LANES, LANES), 1), 1.0, 0.0
    ).astype(bf16)
    upto = dot(present.astype(bf16), tri)
    below = jnp.where(
        lax.broadcasted_iota(i32, (his, his), 0) > lax.broadcasted_iota(i32, (his, his), 1), 1.0, 0.0
    ).astype(bf16)
    totals = jnp.broadcast_to(upto[:, LANES - 1 :], (his, LANES))
    rank = upto - present + dot(below, totals.astype(bf16))
    rank_ref[...] = rank
    rank_cols = jnp.where(present > 0.5, rank, -1.0).T
    lane = lax.broadcasted_iota(i32, (LANES, LANES), 1).astype(f32)
    sub = lax.broadcasted_iota(i32, (LANES, LANES), 0).astype(f32)
    listed = jnp.zeros((LANES, LANES), f32)
    for h in range(his):
        listed = listed + jnp.where(rank_cols[:, h : h + 1] == lane, sub + float(h * LANES), 0.0)
    row = jnp.sum(listed, axis=0, keepdims=True).astype(i32)
    list_ref[...] = jnp.broadcast_to(row, list_ref.shape)


def list_call(loc, groups):
    return pl.pallas_call(
        list_kernel,
        out_shape=(
            jax.ShapeDtypeStruct((groups, LANES), i32),
            jax.ShapeDtypeStruct((ROWS_DEV // LANES, LANES), f32),
        ),
        compiler_params=params(16),
        cost_estimate=cost(1 << 31),
    )(loc)


def map_kernel(own_ref, loc_ref, w_ref, rank_ref, u_ref, c_ref):
    fields, bag_len, samples = own_ref.shape
    groups = u_ref.shape[0]
    rank_b = rank_ref[...].astype(bf16)
    own_iota = lax.broadcasted_iota(i32, (groups, samples), 0)

    def field(f, carry):
        loc, own, w = loc_ref[f], own_ref[f], w_ref[f]
        wsum = jnp.sum(w, axis=0, keepdims=True)
        u_map = jnp.full((groups, samples), -1.0, f32)
        c_map = jnp.zeros((groups, samples), f32)
        for j in range(bag_len):
            lo, hi = marks_of(loc[j : j + 1], samples)
            u = jnp.sum(dot(rank_b, lo) * hi, axis=0, keepdims=True)
            here = own_iota == own[j : j + 1]
            u_map = jnp.where(here, u, u_map)
            c_map = jnp.where(here, w[j : j + 1] / wsum, c_map)
        cols = pl.ds(pl.multiple_of(f * samples, samples), samples)
        u_ref[:, cols] = u_map
        c_ref[:, cols] = c_map
        return carry

    lax.fori_loop(0, fields, field, 0)


def map_call(own, loc, w, rank, groups):
    fields, _, samples = own.shape
    bags = fields * samples
    return pl.pallas_call(
        map_kernel,
        out_shape=(
            jax.ShapeDtypeStruct((groups, bags), f32),
            jax.ShapeDtypeStruct((groups, bags), f32),
        ),
        compiler_params=params(16),
        cost_estimate=cost(1 << 31),
    )(own, loc, w, rank)


def take_kernel(flat_ref, tb_ref, out_ref, tt_ref):
    rows, width = tb_ref.shape
    n = flat_ref.shape[1]

    @pl.when(pl.program_id(0) == 0)
    def _():
        tt_ref[...] = tb_ref[...].T.astype(bf16)

    part = 256
    for k in range(0, n, part):
        asked = flat_ref[:, k : k + part]
        marks = jnp.where(lax.broadcasted_iota(i32, (rows, part), 0) == asked, 1.0, 0.0).astype(bf16)
        out_ref[k : k + part, :] = dot(tt_ref[...], marks).T.astype(bf16)


def take_call(flat, table):
    n = flat.shape[1]
    rows, width = table.shape
    block = TAKE_BLOCK if n % TAKE_BLOCK == 0 else n
    return pl.pallas_call(
        take_kernel,
        grid=(n // block,),
        in_specs=[
            pl.BlockSpec((1, block), lambda i: (0, i)),
            pl.BlockSpec((rows, width), lambda i: (0, 0)),
        ],
        out_specs=pl.BlockSpec((block, width), lambda i: (i, 0)),
        out_shape=jax.ShapeDtypeStruct((n, width), bf16),
        scratch_shapes=[pltpu.VMEM((width, rows), bf16)],
        compiler_params=params(STEP_MIB, ("arbitrary",)),
        cost_estimate=cost(2 * n * rows * width * 2),
    )(flat, table)


def build(u_ref, c_ref, cols, first, count, lo, hi):
    n = hi - lo
    iota = lax.broadcasted_iota(i32, (n, cols.stop - cols.start), 0).astype(f32) + float(lo)
    return jnp.concatenate(
        [
            jnp.where(iota == u_ref[o : o + 1, cols], c_ref[o : o + 1, cols], 0.0)
            for o in range(first, first + count)
        ],
        axis=0,
    ).astype(bf16)


def steps_of(groups, most):
    return min(most, groups)


def pool_kernel(fields, lo, hi, first, last, u_ref, c_ref, r_ref, *refs):
    per_step, bags = u_ref.shape
    samples = bags // fields
    width = r_ref.shape[1]
    x_ref, acc_ref = refs[-2:] if last else (None, refs[-1])

    @pl.when(pl.program_id(0) == 0)
    def _():
        acc_ref[...] = jnp.zeros_like(acc_ref) if first else refs[0][...]

    rt = r_ref[...].astype(f32).T.astype(bf16)
    for f in range(fields):
        cols = slice(f * samples, (f + 1) * samples)
        acc_ref[:, cols] += dot(rt, build(u_ref, c_ref, cols, 0, per_step, lo, hi))

    if last:

        @pl.when(pl.program_id(0) == pl.num_programs(0) - 1)
        def _():
            for f in range(fields):
                x_ref[:, f * width : (f + 1) * width] = acc_ref[:, f * samples : (f + 1) * samples].T.astype(bf16)


def pool_call(u, c, r, fields, lo, hi, prev, last):
    groups, bags = u.shape
    width = r.shape[1]
    per_step = steps_of(groups, POOL_STEP)
    n = hi - lo
    acc = jax.ShapeDtypeStruct((width, bags), f32)
    x = jax.ShapeDtypeStruct((bags // fields, fields * width), bf16)
    acc_spec = pl.BlockSpec((width, bags), lambda i: (0, 0))
    return pl.pallas_call(
        functools.partial(pool_kernel, fields, lo, hi, prev is None, last),
        grid=(groups // per_step,),
        in_specs=[
            pl.BlockSpec((per_step, bags), lambda i: (i, 0)),
            pl.BlockSpec((per_step, bags), lambda i: (i, 0)),
            pl.BlockSpec((per_step * n, width), lambda i: (i, 0)),
        ]
        + ([] if prev is None else [acc_spec]),
        out_specs=pl.BlockSpec(x.shape, lambda i: (0, 0)) if last else acc_spec,
        out_shape=x if last else acc,
        scratch_shapes=[pltpu.VMEM((width, bags), f32)] if last else [],
        compiler_params=params(56, ("arbitrary",)),
        cost_estimate=cost(1<<34, 0),
    )(u, c, r, *([] if prev is None else [prev]))


def head_kernel(core_ref, x_ref, lab_ref, bw_ref, own_ref, near_ref, other_ref, far_ref, rest_ref, *refs):
    dt_ref, d_ref, slope_ref, acc_ref, held, sem = refs
    samples, ins = x_ref.shape
    width = d_ref.shape[1]
    hidden = own_ref.shape[1]
    half = far_ref.shape[0]
    core = core_ref[0]
    places = [
        (own_ref, held.at[0]),
        (near_ref, held.at[1]),
        (other_ref, held.at[2]),
        (far_ref, held.at[3, pl.ds(pl.multiple_of(core * half, half), half)]),
        (rest_ref, held.at[3, pl.ds(pl.multiple_of((1 - core) * half, half), half)]),
    ]
    copies = [pltpu.make_async_copy(a, b, sem.at[k]) for k, (a, b) in enumerate(places)]
    for copy in copies:
        copy.start()
    x = x_ref[...]
    logits = jnp.zeros((samples, 1), f32)
    cut = HEAD_CUT
    parts = [(b, slice(c, c + cut)) for b in range(4) for c in range(0, hidden, cut)]
    pre = None
    for k in range(len(parts) + 1):
        done = pre
        if k < len(parts):
            b, cols = parts[k]
            if cols.start == 0:
                copies[b].wait()
                if b == 3:
                    copies[4].wait()
            pre = dot(x, held[b, :, cols]) + bw_ref[b * TAIL : b * TAIL + 1, cols].astype(f32)
        if k > 0:
            b, cols = parts[k - 1]
            out = bw_ref[b * TAIL + 1 : b * TAIL + 2, cols].astype(f32)
            sig = jax.nn.sigmoid(done)
            logits = logits + jnp.sum(done * sig * out, axis=1, keepdims=True)
            slope_ref[b, :, cols] = (out * (sig * (1.0 + done * (1.0 - sig)))).astype(bf16)
    logits = jnp.broadcast_to(logits, (samples, LANES)).T[:1, :]
    grad = jax.nn.sigmoid(logits) - lab_ref[...]
    for b in range(4):
        part = dot(held[b], slope_ref[b], ((1,), (1,)))
        acc_ref[...] = part if b == 0 else acc_ref[...] + part
    for f in range(ins // width):
        block = acc_ref[f * width : (f + 1) * width, :] * grad
        dt_ref[f * width : (f + 1) * width, :] = block.astype(bf16)
        d_ref[f * samples : (f + 1) * samples, :] = block.T.astype(bf16)


def head_call(core, x, labels, bw, weights, width):
    samples, ins = x.shape
    hidden = weights[0].shape[1]
    vmem = pl.BlockSpec(memory_space=pltpu.VMEM)
    return pl.pallas_call(
        head_kernel,
        in_specs=[pl.BlockSpec(memory_space=pltpu.SMEM), vmem, vmem, vmem]
        + [pl.BlockSpec(memory_space=pl.ANY)] * len(weights),
        out_specs=(vmem, vmem),
        out_shape=(
            jax.ShapeDtypeStruct((ins, samples), bf16),
            jax.ShapeDtypeStruct((ins // width * samples, width), bf16),
        ),
        scratch_shapes=[
            pltpu.VMEM((4, samples, hidden), bf16),
            pltpu.VMEM((ins, samples), f32),
            pltpu.VMEM((4, ins, hidden), bf16),
            pltpu.SemaphoreType.DMA((len(weights),)),
        ],
        compiler_params=params(HEAD_MIB),
        cost_estimate=cost(4 * samples * ins * hidden * 4, 14 << 20),
    )(core, x, labels, bw, *weights)


def give_kernel(fields, lo, hi, u_ref, c_ref, d_ref, g_ref):
    per_step, bags = u_ref.shape
    samples = bags // fields
    total = None
    for f in range(fields):
        cols = slice(f * samples, (f + 1) * samples)
        got = dot(build(u_ref, c_ref, cols, 0, per_step, lo, hi), d_ref[cols, :])
        total = got if total is None else total + got
    g_ref[...] = total.astype(bf16)


def give_call(u, c, d, fields, lo, hi):
    groups, bags = u.shape
    width = d.shape[1]
    per_step = steps_of(groups, GIVE_STEP)
    n = hi - lo
    return pl.pallas_call(
        functools.partial(give_kernel, fields, lo, hi),
        grid=(groups // per_step,),
        in_specs=[
            pl.BlockSpec((per_step, bags), lambda i: (i, 0)),
            pl.BlockSpec((per_step, bags), lambda i: (i, 0)),
            pl.BlockSpec((bags, width), lambda i: (0, 0)),
        ],
        out_specs=pl.BlockSpec((per_step * n, width), lambda i: (i, 0)),
        out_shape=jax.ShapeDtypeStruct((groups * n, width), bf16),
        compiler_params=params(STEP_MIB, ("arbitrary",)),
        cost_estimate=cost(2 * groups * n * bags * width * 2),
    )(u, c, d)


def along_kernel(own_ref, w_ref, u_ref, dt_ref, *refs):
    r_refs, (out_ref, acc_ref) = refs[:-2], refs[-2:]
    fields, bag_len, samples = own_ref.shape
    per_step = u_ref.shape[0]
    width = r_refs[0].shape[1]
    step = pl.program_id(0)

    @pl.when(step == 0)
    def _():
        acc_ref[...] = jnp.zeros_like(acc_ref)

    def field(f, carry):
        cols = pl.ds(pl.multiple_of(f * samples, samples), samples)
        d = dt_ref[pl.ds(pl.multiple_of(f * width, width), width), :]
        prods = [dot(r_ref[...], d) for r_ref in r_refs]
        u = u_ref[:, cols]
        own = own_ref[f]
        got = acc_ref[f]
        for o in range(per_step):
            value = None
            for (lo, hi), prod in zip(CHUNKS, prods):
                n = hi - lo
                iota = lax.broadcasted_iota(i32, (n, samples), 0).astype(f32) + float(lo)
                hit = jnp.where(iota == u[o : o + 1], prod[o * n : (o + 1) * n, :], 0.0)
                part = jnp.sum(hit.reshape(n // 8, 8, samples), axis=0)
                value = part if value is None else value + part
            value = jnp.sum(value, axis=0, keepdims=True)
            got = jnp.where(own == step * per_step + o, value, got)
        acc_ref[f] = got
        return carry

    lax.fori_loop(0, fields, field, 0)

    @pl.when(step == pl.num_programs(0) - 1)
    def _():
        for f in range(fields):
            w = w_ref[f]
            wsum = jnp.sum(w, axis=0, keepdims=True)
            along = acc_ref[f]
            centre = jnp.sum(w * along, axis=0, keepdims=True) / wsum
            out_ref[f] = (along - centre) / wsum


def along_call(own, w, u, dt, rs):
    groups, bags = u.shape
    width = rs[0].shape[1]
    per_step = steps_of(groups, ALONG_STEP)
    whole3 = pl.BlockSpec(own.shape, lambda i: (0, 0, 0))
    return pl.pallas_call(
        along_kernel,
        grid=(groups // per_step,),
        in_specs=[
            whole3,
            whole3,
            pl.BlockSpec((per_step, bags), lambda i: (i, 0)),
            pl.BlockSpec(dt.shape, lambda i: (0, 0)),
        ]
        + [pl.BlockSpec((per_step * (hi - lo), width), lambda i: (i, 0)) for lo, hi in CHUNKS],
        out_specs=whole3,
        out_shape=jax.ShapeDtypeStruct(own.shape, f32),
        scratch_shapes=[pltpu.VMEM(own.shape, f32)],
        compiler_params=params(STEP_MIB, ("arbitrary",)),
        cost_estimate=cost(2 * groups * UNIQ * bags * width * 2),
    )(own, w, u, dt, *rs)


def add_kernel(first, last, lo, hi, list_ref, g_ref, *refs):
    out_ref, acc_ref = refs[-2:] if last else (None, refs[-1])
    width, rows = acc_ref.shape
    per_step = list_ref.shape[0]

    @pl.when(pl.program_id(0) == 0)
    def _():
        acc_ref[...] = jnp.zeros_like(acc_ref) if first else refs[0][...]

    asked = list_ref[...].T
    columns = jnp.concatenate([asked[lo:hi, o : o + 1] for o in range(per_step)], axis=0)
    gt = g_ref[...].astype(f32).T.astype(bf16)
    part = 256
    for k in range(0, rows, part):
        iota = lax.broadcasted_iota(i32, (columns.shape[0], part), 1) + k
        marks = jnp.where(iota == columns, 1.0, 0.0).astype(bf16)
        acc_ref[:, k : k + part] += dot(gt, marks)

    if last:

        @pl.when(pl.program_id(0) == pl.num_programs(0) - 1)
        def _():
            for k in range(0, rows, part):
                out_ref[k : k + part, :] = acc_ref[:, k : k + part].T.astype(bf16)


def add_call(lists, g, rows, lo, hi, prev, last):
    groups = lists.shape[0]
    width = g.shape[1]
    per_step = steps_of(groups, ADD_STEP)
    acc = pl.BlockSpec((width, rows), lambda i: (0, 0))
    return pl.pallas_call(
        functools.partial(add_kernel, prev is None, last, lo, hi),
        grid=(groups // per_step,),
        in_specs=[
            pl.BlockSpec((per_step, LANES), lambda i: (i, 0)),
            pl.BlockSpec((per_step * (hi - lo), width), lambda i: (i, 0)),
        ]
        + ([] if prev is None else [acc]),
        out_specs=pl.BlockSpec((rows, width), lambda i: (0, 0)) if last else acc,
        out_shape=jax.ShapeDtypeStruct((rows, width), bf16) if last else jax.ShapeDtypeStruct((width, rows), f32),
        scratch_shapes=[pltpu.VMEM((width, rows), f32)] if last else [],
        compiler_params=params(STEP_MIB, ("arbitrary",)),
        cost_estimate=cost(2 * g.shape[0] * rows * width * 2),
    )(lists, g, *([] if prev is None else [prev]))


def send(x, groups):
    width = x.shape[1]
    return lax.all_to_all(
        x.reshape(groups, -1, width), "owner", split_axis=0, concat_axis=0, tiled=True
    ).reshape(-1, width)


def turn(x, shift):
    dense = lax.axis_size("dense")
    return lax.ppermute(x, "dense", [(i, (i + shift) % dense) for i in range(dense)])


def hop(x):
    groups, dense = lax.axis_size("owner"), lax.axis_size("dense")
    pairs = [(o * dense + q, o * dense + (q + 1 - 2 * (o % 2)) % dense) for o in range(groups) for q in range(dense)]
    return lax.ppermute(x, ("owner", "dense"), pairs)


def swap(x):
    return lax.ppermute(x, "owner", [(i, i ^ 1) for i in range(lax.axis_size("owner"))])


def local(owners, local_rows, weights, labels, table, accum, w_in, b_in, w_out):
    fields = owners.shape[1]
    rows, width = table.shape
    groups = lax.axis_size("owner")
    dense = lax.axis_size("dense")
    own, loc, w = (a.transpose(1, 2, 0) for a in (owners, local_rows, weights))

    near = hop(w_in)
    listed, rank = list_call(loc, groups)
    lists = lax.all_to_all(listed, "owner", split_axis=0, concat_axis=0, tiled=True)
    flat = [lists[:, lo:hi].reshape(1, groups * (hi - lo)) for lo, hi in CHUNKS]
    found = [take_call(a, table) for a in flat]
    rs = [send(x, groups) for x in found]
    u, c = map_call(own, loc, w, after(rank, *found), groups)

    core = (lax.axis_index("owner") % 2).astype(i32)
    half = w_in.shape[0] // 2
    near = after(near, u)
    far = hop(lax.dynamic_slice_in_dim(near, core * half, half, axis=0))
    bw = jnp.concatenate([b_in[None], w_out[None], jnp.zeros((TAIL - 2, w_in.shape[1]), bf16)], axis=0)
    bw = after(bw, u)
    bw_near = hop(bw)
    bw = jnp.concatenate([bw, bw_near, swap(bw_near), hop(bw_near)], axis=0)
    other = swap(near)
    rest = swap(far)
    head_weights = [w_in, near, other, far, rest]

    x = None
    for k, (lo, hi) in enumerate(CHUNKS):
        x = pool_call(u, c, after(rs[k], far), fields, lo, hi, x, k == len(CHUNKS) - 1)
    dt, d = head_call(core[None], x, labels.astype(f32)[None], bw, head_weights, width)
    gs = [give_call(u, c, d, fields, lo, hi) for lo, hi in CHUNKS]
    gots = [send(g, groups) for g in gs]
    weight_grad = along_call(own, w, u, after(dt, *gs), rs)
    part = None
    for k, (lo, hi) in enumerate(CHUNKS):
        got = after(gots[k], weight_grad) if k == 0 else gots[k]
        part = add_call(lists, got, rows, lo, hi, part, k == len(CHUNKS) - 1)

    cut = rows // dense
    me = lax.axis_index("dense")
    piece = lambda k: lax.dynamic_slice_in_dim(part, lax.rem(me + k, dense) * cut, cut, axis=0)
    total = piece(0).astype(f32)
    for k in range(1, dense):
        total = total + turn(piece(k), k).astype(f32)
    total = total.astype(bf16)
    row_grad = jnp.zeros((rows, width), bf16)
    for k in range(dense):
        got = total if k == 0 else turn(total, k)
        row_grad = lax.dynamic_update_slice_in_dim(row_grad, got, lax.rem(me + dense - k, dense) * cut, axis=0)
    row_grad = row_grad.astype(f32)
    new_accum = accum + jnp.mean(row_grad * row_grad, axis=-1)
    new_table = table - step_size * row_grad / jnp.sqrt(new_accum)[:, None]
    return (new_table, new_accum, weight_grad.transpose(2, 0, 1))


def solution(mesh):
    placed = (
        P(("owner", "dense"), None, None),
        P(("owner", "dense"), None, None),
        P(("owner", "dense"), None, None),
        P(("owner", "dense")),
        P("owner", None),
        P("owner"),
        P(None, "dense"),
        P("dense"),
        P("dense"),
    )
    return jax.shard_map(
        local,
        mesh=mesh,
        in_specs=placed,
        out_specs=(P("owner", None), P("owner"), P(("owner", "dense"), None, None)),
        check_vma=False,
    )
```

```python
import functools

import jax
import jax.numpy as jnp
from jax import lax
from jax.experimental import pallas as pl
from jax.experimental.pallas import tpu as pltpu
from jax.sharding import PartitionSpec as P

step_size = 0.5
UNIQ = 104
ROWS_DEV = 2048
LANES = 128
CHUNKS = ((0, 104),)
TAIL = 16
TAKE_BLOCK, POOL_STEP, GIVE_STEP, ADD_STEP, ALONG_STEP = 3328, 32, 16, 32, 8
HEAD_CUT, HEAD_MIB, STEP_MIB = 1024, 36, 32
MIB = 1024 * 1024
f32, bf16, i32 = jnp.float32, jnp.bfloat16, jnp.int32


def dot(a, b, dims=((1,), (0,))):
    return lax.dot_general(a, b, (dims, ((), ())), preferred_element_type=f32)


def params(mib, sem=None):
    return pltpu.CompilerParams(vmem_limit_bytes=mib * MIB, dimension_semantics=sem)


def cost(flops, moved=1 << 20):
    if moved == 0:
        return pl.CostEstimate(flops=flops, bytes_accessed=1 << 10, transcendentals=0)
    return pl.CostEstimate(flops=1 << 20, bytes_accessed=1 << 10, transcendentals=0)


def after(x, *before):
    return lax.optimization_barrier((x, *before))[0]


def marks_of(row, samples):
    lo = lax.broadcasted_iota(i32, (LANES, samples), 0) == (row & (LANES - 1))
    hi = lax.broadcasted_iota(i32, (ROWS_DEV // LANES, samples), 0) == (row >> 7)
    return jnp.where(lo, 1.0, 0.0).astype(bf16), jnp.where(hi, 1.0, 0.0)


def list_kernel(loc_ref, list_ref, rank_ref):
    fields, bag_len, samples = loc_ref.shape
    his = ROWS_DEV // LANES
    count = jnp.zeros((his, LANES), f32)
    for f in range(fields):
        for j in range(bag_len):
            lo, hi = marks_of(loc_ref[f, j : j + 1, :], samples)
            count = count + dot(hi.astype(bf16), lo, ((1,), (1,)))
    present = jnp.where(count > 0.5, 1.0, 0.0)
    tri = jnp.where(
        lax.broadcasted_iota(i32, (LANES, LANES), 0) <= lax.broadcasted_iota(i32, (LANES, LANES), 1), 1.0, 0.0
    ).astype(bf16)
    upto = dot(present.astype(bf16), tri)
    below = jnp.where(
        lax.broadcasted_iota(i32, (his, his), 0) > lax.broadcasted_iota(i32, (his, his), 1), 1.0, 0.0
    ).astype(bf16)
    totals = jnp.broadcast_to(upto[:, LANES - 1 :], (his, LANES))
    rank = upto - present + dot(below, totals.astype(bf16))
    rank_ref[...] = rank
    rank_cols = jnp.where(present > 0.5, rank, -1.0).T
    lane = lax.broadcasted_iota(i32, (LANES, LANES), 1).astype(f32)
    sub = lax.broadcasted_iota(i32, (LANES, LANES), 0).astype(f32)
    listed = jnp.zeros((LANES, LANES), f32)
    for h in range(his):
        listed = listed + jnp.where(rank_cols[:, h : h + 1] == lane, sub + float(h * LANES), 0.0)
    row = jnp.sum(listed, axis=0, keepdims=True).astype(i32)
    list_ref[...] = jnp.broadcast_to(row, list_ref.shape)


def list_call(loc, groups):
    return pl.pallas_call(
        list_kernel,
        out_shape=(
            jax.ShapeDtypeStruct((groups, LANES), i32),
            jax.ShapeDtypeStruct((ROWS_DEV // LANES, LANES), f32),
        ),
        compiler_params=params(16),
        cost_estimate=cost(1 << 31),
    )(loc)


def map_kernel(own_ref, loc_ref, w_ref, rank_ref, u_ref, c_ref):
    fields, bag_len, samples = own_ref.shape
    groups = u_ref.shape[0]
    rank_b = rank_ref[...].astype(bf16)
    own_iota = lax.broadcasted_iota(i32, (groups, samples), 0)

    def field(f, carry):
        loc, own, w = loc_ref[f], own_ref[f], w_ref[f]
        wsum = jnp.sum(w, axis=0, keepdims=True)
        u_map = jnp.full((groups, samples), -1.0, f32)
        c_map = jnp.zeros((groups, samples), f32)
        for j in range(bag_len):
            lo, hi = marks_of(loc[j : j + 1], samples)
            u = jnp.sum(dot(rank_b, lo) * hi, axis=0, keepdims=True)
            here = own_iota == own[j : j + 1]
            u_map = jnp.where(here, u, u_map)
            c_map = jnp.where(here, w[j : j + 1] / wsum, c_map)
        cols = pl.ds(pl.multiple_of(f * samples, samples), samples)
        u_ref[:, cols] = u_map
        c_ref[:, cols] = c_map
        return carry

    lax.fori_loop(0, fields, field, 0)


def map_call(own, loc, w, rank, groups):
    fields, _, samples = own.shape
    bags = fields * samples
    return pl.pallas_call(
        map_kernel,
        out_shape=(
            jax.ShapeDtypeStruct((groups, bags), f32),
            jax.ShapeDtypeStruct((groups, bags), f32),
        ),
        compiler_params=params(16),
        cost_estimate=cost(1 << 31),
    )(own, loc, w, rank)


def turned_kernel(table_ref, list_ref, out_ref):
    out_ref[...] = table_ref[...].T.astype(bf16)


def turned_call(table, listed):
    rows, width = table.shape
    vmem = pl.BlockSpec(memory_space=pltpu.VMEM)
    return pl.pallas_call(
        turned_kernel,
        in_specs=[vmem, pl.BlockSpec(memory_space=pl.ANY)],
        out_specs=vmem,
        out_shape=jax.ShapeDtypeStruct((width, rows), bf16),
        compiler_params=params(16),
        cost_estimate=cost(1 << 31),
    )(table, listed)


def take_kernel(flat_ref, tt_ref, out_ref):
    rows = tt_ref.shape[1]
    n = flat_ref.shape[1]
    part = 256
    for k in range(0, n, part):
        asked = flat_ref[:, k : k + part]
        marks = jnp.where(lax.broadcasted_iota(i32, (rows, part), 0) == asked, 1.0, 0.0).astype(bf16)
        out_ref[k : k + part, :] = dot(tt_ref[...], marks).T.astype(bf16)


def take_call(flat, tt):
    n = flat.shape[1]
    width, rows = tt.shape
    block = TAKE_BLOCK if n % TAKE_BLOCK == 0 else n
    return pl.pallas_call(
        take_kernel,
        grid=(n // block,),
        in_specs=[
            pl.BlockSpec((1, block), lambda i: (0, i)),
            pl.BlockSpec((width, rows), lambda i: (0, 0)),
        ],
        out_specs=pl.BlockSpec((block, width), lambda i: (i, 0)),
        out_shape=jax.ShapeDtypeStruct((n, width), bf16),
        compiler_params=params(STEP_MIB, ("arbitrary",)),
        cost_estimate=cost(2 * n * rows * width * 2),
    )(flat, tt)


def build(u_ref, c_ref, cols, first, count, lo, hi):
    n = hi - lo
    iota = lax.broadcasted_iota(i32, (n, cols.stop - cols.start), 0).astype(f32) + float(lo)
    return jnp.concatenate(
        [
            jnp.where(iota == u_ref[o : o + 1, cols], c_ref[o : o + 1, cols], 0.0)
            for o in range(first, first + count)
        ],
        axis=0,
    ).astype(bf16)


def steps_of(groups, most):
    return min(most, groups)


def pool_kernel(fields, lo, hi, first, last, u_ref, c_ref, r_ref, *refs):
    per_step, bags = u_ref.shape
    samples = bags // fields
    width = r_ref.shape[1]
    x_ref, acc_ref = refs[-2:] if last else (None, refs[-1])

    @pl.when(pl.program_id(0) == 0)
    def _():
        acc_ref[...] = jnp.zeros_like(acc_ref) if first else refs[0][...]

    rt = r_ref[...].astype(f32).T.astype(bf16)
    for f in range(fields):
        cols = slice(f * samples, (f + 1) * samples)
        acc_ref[:, cols] += dot(rt, build(u_ref, c_ref, cols, 0, per_step, lo, hi))

    if last:

        @pl.when(pl.program_id(0) == pl.num_programs(0) - 1)
        def _():
            for f in range(fields):
                x_ref[:, f * width : (f + 1) * width] = acc_ref[:, f * samples : (f + 1) * samples].T.astype(bf16)


def pool_call(u, c, r, fields, lo, hi, prev, last):
    groups, bags = u.shape
    width = r.shape[1]
    per_step = steps_of(groups, POOL_STEP)
    n = hi - lo
    acc = jax.ShapeDtypeStruct((width, bags), f32)
    x = jax.ShapeDtypeStruct((bags // fields, fields * width), bf16)
    acc_spec = pl.BlockSpec((width, bags), lambda i: (0, 0))
    return pl.pallas_call(
        functools.partial(pool_kernel, fields, lo, hi, prev is None, last),
        grid=(groups // per_step,),
        in_specs=[
            pl.BlockSpec((per_step, bags), lambda i: (i, 0)),
            pl.BlockSpec((per_step, bags), lambda i: (i, 0)),
            pl.BlockSpec((per_step * n, width), lambda i: (i, 0)),
        ]
        + ([] if prev is None else [acc_spec]),
        out_specs=pl.BlockSpec(x.shape, lambda i: (0, 0)) if last else acc_spec,
        out_shape=x if last else acc,
        scratch_shapes=[pltpu.VMEM((width, bags), f32)] if last else [],
        compiler_params=params(56, ("arbitrary",)),
        cost_estimate=cost(1<<34, 0),
    )(u, c, r, *([] if prev is None else [prev]))


def head_kernel(core_ref, x_ref, lab_ref, bw_ref, own_ref, near_ref, other_ref, far_ref, rest_ref, *refs):
    dt_ref, d_ref, slope_ref, acc_ref, held, sem = refs
    samples, ins = x_ref.shape
    width = d_ref.shape[1]
    hidden = own_ref.shape[1]
    half = far_ref.shape[0]
    core = core_ref[0]
    places = [
        (own_ref, held.at[0]),
        (near_ref, held.at[1]),
        (other_ref, held.at[2]),
        (far_ref, held.at[3, pl.ds(pl.multiple_of(core * half, half), half)]),
        (rest_ref, held.at[3, pl.ds(pl.multiple_of((1 - core) * half, half), half)]),
    ]
    copies = [pltpu.make_async_copy(a, b, sem.at[k]) for k, (a, b) in enumerate(places)]
    for copy in copies:
        copy.start()
    x = x_ref[...]
    logits = jnp.zeros((samples, 1), f32)
    cut = HEAD_CUT
    parts = [(b, slice(c, c + cut)) for b in range(4) for c in range(0, hidden, cut)]
    pre = None
    for k in range(len(parts) + 1):
        done = pre
        if k < len(parts):
            b, cols = parts[k]
            if cols.start == 0:
                copies[b].wait()
                if b == 3:
                    copies[4].wait()
            pre = dot(x, held[b, :, cols]) + bw_ref[b * TAIL : b * TAIL + 1, cols].astype(f32)
        if k > 0:
            b, cols = parts[k - 1]
            out = bw_ref[b * TAIL + 1 : b * TAIL + 2, cols].astype(f32)
            sig = jax.nn.sigmoid(done)
            logits = logits + jnp.sum(done * sig * out, axis=1, keepdims=True)
            slope_ref[b, :, cols] = (out * (sig * (1.0 + done * (1.0 - sig)))).astype(bf16)
    logits = jnp.broadcast_to(logits, (samples, LANES)).T[:1, :]
    grad = jax.nn.sigmoid(logits) - lab_ref[...]
    for b in range(4):
        part = dot(held[b], slope_ref[b], ((1,), (1,)))
        acc_ref[...] = part if b == 0 else acc_ref[...] + part
    for f in range(ins // width):
        block = acc_ref[f * width : (f + 1) * width, :] * grad
        dt_ref[f * width : (f + 1) * width, :] = block.astype(bf16)
        d_ref[f * samples : (f + 1) * samples, :] = block.T.astype(bf16)


def head_call(core, x, labels, bw, weights, width):
    samples, ins = x.shape
    hidden = weights[0].shape[1]
    vmem = pl.BlockSpec(memory_space=pltpu.VMEM)
    return pl.pallas_call(
        head_kernel,
        in_specs=[pl.BlockSpec(memory_space=pltpu.SMEM), vmem, vmem, vmem]
        + [pl.BlockSpec(memory_space=pl.ANY)] * len(weights),
        out_specs=(vmem, vmem),
        out_shape=(
            jax.ShapeDtypeStruct((ins, samples), bf16),
            jax.ShapeDtypeStruct((ins // width * samples, width), bf16),
        ),
        scratch_shapes=[
            pltpu.VMEM((4, samples, hidden), bf16),
            pltpu.VMEM((ins, samples), f32),
            pltpu.VMEM((4, ins, hidden), bf16),
            pltpu.SemaphoreType.DMA((len(weights),)),
        ],
        compiler_params=params(HEAD_MIB),
        cost_estimate=cost(4 * samples * ins * hidden * 4, 14 << 20),
    )(core, x, labels, bw, *weights)


def give_kernel(fields, lo, hi, u_ref, c_ref, d_ref, g_ref):
    per_step, bags = u_ref.shape
    samples = bags // fields
    total = None
    for f in range(fields):
        cols = slice(f * samples, (f + 1) * samples)
        got = dot(build(u_ref, c_ref, cols, 0, per_step, lo, hi), d_ref[cols, :])
        total = got if total is None else total + got
    g_ref[...] = total.astype(bf16)


def give_call(u, c, d, fields, lo, hi):
    groups, bags = u.shape
    width = d.shape[1]
    per_step = steps_of(groups, GIVE_STEP)
    n = hi - lo
    return pl.pallas_call(
        functools.partial(give_kernel, fields, lo, hi),
        grid=(groups // per_step,),
        in_specs=[
            pl.BlockSpec((per_step, bags), lambda i: (i, 0)),
            pl.BlockSpec((per_step, bags), lambda i: (i, 0)),
            pl.BlockSpec((bags, width), lambda i: (0, 0)),
        ],
        out_specs=pl.BlockSpec((per_step * n, width), lambda i: (i, 0)),
        out_shape=jax.ShapeDtypeStruct((groups * n, width), bf16),
        compiler_params=params(STEP_MIB, ("arbitrary",)),
        cost_estimate=cost(2 * groups * n * bags * width * 2),
    )(u, c, d)


def along_kernel(own_ref, w_ref, u_ref, dt_ref, *refs):
    r_refs, (out_ref, acc_ref) = refs[:-2], refs[-2:]
    fields, bag_len, samples = own_ref.shape
    per_step = u_ref.shape[0]
    width = r_refs[0].shape[1]
    step = pl.program_id(0)

    @pl.when(step == 0)
    def _():
        acc_ref[...] = jnp.zeros_like(acc_ref)

    def field(f, carry):
        cols = pl.ds(pl.multiple_of(f * samples, samples), samples)
        d = dt_ref[pl.ds(pl.multiple_of(f * width, width), width), :]
        prods = [dot(r_ref[...], d) for r_ref in r_refs]
        u = u_ref[:, cols]
        own = own_ref[f]
        got = acc_ref[f]
        for o in range(per_step):
            value = None
            for (lo, hi), prod in zip(CHUNKS, prods):
                n = hi - lo
                iota = lax.broadcasted_iota(i32, (n, samples), 0).astype(f32) + float(lo)
                hit = jnp.where(iota == u[o : o + 1], prod[o * n : (o + 1) * n, :], 0.0)
                part = jnp.sum(hit.reshape(n // 8, 8, samples), axis=0)
                value = part if value is None else value + part
            value = jnp.sum(value, axis=0, keepdims=True)
            got = jnp.where(own == step * per_step + o, value, got)
        acc_ref[f] = got
        return carry

    lax.fori_loop(0, fields, field, 0)

    @pl.when(step == pl.num_programs(0) - 1)
    def _():
        for f in range(fields):
            w = w_ref[f]
            wsum = jnp.sum(w, axis=0, keepdims=True)
            along = acc_ref[f]
            centre = jnp.sum(w * along, axis=0, keepdims=True) / wsum
            out_ref[f] = (along - centre) / wsum


def along_call(own, w, u, dt, rs):
    groups, bags = u.shape
    width = rs[0].shape[1]
    per_step = steps_of(groups, ALONG_STEP)
    whole3 = pl.BlockSpec(own.shape, lambda i: (0, 0, 0))
    return pl.pallas_call(
        along_kernel,
        grid=(groups // per_step,),
        in_specs=[
            whole3,
            whole3,
            pl.BlockSpec((per_step, bags), lambda i: (i, 0)),
            pl.BlockSpec(dt.shape, lambda i: (0, 0)),
        ]
        + [pl.BlockSpec((per_step * (hi - lo), width), lambda i: (i, 0)) for lo, hi in CHUNKS],
        out_specs=whole3,
        out_shape=jax.ShapeDtypeStruct(own.shape, f32),
        scratch_shapes=[pltpu.VMEM(own.shape, f32)],
        compiler_params=params(STEP_MIB, ("arbitrary",)),
        cost_estimate=cost(2 * groups * UNIQ * bags * width * 2),
    )(own, w, u, dt, *rs)


def add_kernel(first, last, lo, hi, list_ref, g_ref, *refs):
    out_ref, acc_ref = refs[-2:] if last else (None, refs[-1])
    width, rows = acc_ref.shape
    per_step = list_ref.shape[0]

    @pl.when(pl.program_id(0) == 0)
    def _():
        acc_ref[...] = jnp.zeros_like(acc_ref) if first else refs[0][...]

    asked = list_ref[...].T
    columns = jnp.concatenate([asked[lo:hi, o : o + 1] for o in range(per_step)], axis=0)
    gt = g_ref[...].astype(f32).T.astype(bf16)
    part = 256
    for k in range(0, rows, part):
        iota = lax.broadcasted_iota(i32, (columns.shape[0], part), 1) + k
        marks = jnp.where(iota == columns, 1.0, 0.0).astype(bf16)
        acc_ref[:, k : k + part] += dot(gt, marks)

    if last:

        @pl.when(pl.program_id(0) == pl.num_programs(0) - 1)
        def _():
            for k in range(0, rows, part):
                out_ref[k : k + part, :] = acc_ref[:, k : k + part].T.astype(bf16)


def add_call(lists, g, rows, lo, hi, prev, last):
    groups = lists.shape[0]
    width = g.shape[1]
    per_step = steps_of(groups, ADD_STEP)
    acc = pl.BlockSpec((width, rows), lambda i: (0, 0))
    return pl.pallas_call(
        functools.partial(add_kernel, prev is None, last, lo, hi),
        grid=(groups // per_step,),
        in_specs=[
            pl.BlockSpec((per_step, LANES), lambda i: (i, 0)),
            pl.BlockSpec((per_step * (hi - lo), width), lambda i: (i, 0)),
        ]
        + ([] if prev is None else [acc]),
        out_specs=pl.BlockSpec((rows, width), lambda i: (0, 0)) if last else acc,
        out_shape=jax.ShapeDtypeStruct((rows, width), bf16) if last else jax.ShapeDtypeStruct((width, rows), f32),
        scratch_shapes=[pltpu.VMEM((width, rows), f32)] if last else [],
        compiler_params=params(STEP_MIB, ("arbitrary",)),
        cost_estimate=cost(2 * g.shape[0] * rows * width * 2),
    )(lists, g, *([] if prev is None else [prev]))


def send(x, groups):
    width = x.shape[1]
    return lax.all_to_all(
        x.reshape(groups, -1, width), "owner", split_axis=0, concat_axis=0, tiled=True
    ).reshape(-1, width)


def turn(x, shift):
    dense = lax.axis_size("dense")
    return lax.ppermute(x, "dense", [(i, (i + shift) % dense) for i in range(dense)])


def hop(x):
    groups, dense = lax.axis_size("owner"), lax.axis_size("dense")
    pairs = [(o * dense + q, o * dense + (q + 1 - 2 * (o % 2)) % dense) for o in range(groups) for q in range(dense)]
    return lax.ppermute(x, ("owner", "dense"), pairs)


def swap(x):
    return lax.ppermute(x, "owner", [(i, i ^ 1) for i in range(lax.axis_size("owner"))])


def local(owners, local_rows, weights, labels, table, accum, w_in, b_in, w_out):
    fields = owners.shape[1]
    rows, width = table.shape
    groups = lax.axis_size("owner")
    dense = lax.axis_size("dense")
    own, loc, w = (a.transpose(1, 2, 0) for a in (owners, local_rows, weights))

    near = hop(w_in)
    listed, rank = list_call(loc, groups)
    lists = lax.all_to_all(listed, "owner", split_axis=0, concat_axis=0, tiled=True)
    tt = turned_call(table, listed)
    flat = [lists[:, lo:hi].reshape(1, groups * (hi - lo)) for lo, hi in CHUNKS]
    found = [take_call(a, tt) for a in flat]
    rs = [send(x, groups) for x in found]
    u, c = map_call(own, loc, w, after(rank, *found), groups)

    core = (lax.axis_index("owner") % 2).astype(i32)
    half = w_in.shape[0] // 2
    near = after(near, u)
    far = hop(lax.dynamic_slice_in_dim(near, core * half, half, axis=0))
    bw = jnp.concatenate([b_in[None], w_out[None], jnp.zeros((TAIL - 2, w_in.shape[1]), bf16)], axis=0)
    bw = after(bw, u)
    bw_near = hop(bw)
    bw = jnp.concatenate([bw, bw_near, swap(bw_near), hop(bw_near)], axis=0)
    other = swap(near)
    rest = swap(far)
    head_weights = [w_in, near, other, far, rest]

    x = None
    for k, (lo, hi) in enumerate(CHUNKS):
        x = pool_call(u, c, after(rs[k], far), fields, lo, hi, x, k == len(CHUNKS) - 1)
    dt, d = head_call(core[None], x, labels.astype(f32)[None], bw, head_weights, width)
    gs = [give_call(u, c, d, fields, lo, hi) for lo, hi in CHUNKS]
    gots = [send(g, groups) for g in gs]
    weight_grad = along_call(own, w, u, after(dt, *gs), rs)
    part = None
    for k, (lo, hi) in enumerate(CHUNKS):
        got = after(gots[k], weight_grad) if k == 0 else gots[k]
        part = add_call(lists, got, rows, lo, hi, part, k == len(CHUNKS) - 1)

    cut = rows // dense
    me = lax.axis_index("dense")
    piece = lambda k: lax.dynamic_slice_in_dim(part, lax.rem(me + k, dense) * cut, cut, axis=0)
    total = piece(0).astype(f32)
    for k in range(1, dense):
        total = total + turn(piece(k), k).astype(f32)
    total = total.astype(bf16)
    row_grad = jnp.zeros((rows, width), bf16)
    for k in range(dense):
        got = total if k == 0 else turn(total, k)
        row_grad = lax.dynamic_update_slice_in_dim(row_grad, got, lax.rem(me + dense - k, dense) * cut, axis=0)
    row_grad = row_grad.astype(f32)
    new_accum = accum + jnp.mean(row_grad * row_grad, axis=-1)
    new_table = table - step_size * row_grad / jnp.sqrt(new_accum)[:, None]
    return (new_table, new_accum, weight_grad.transpose(2, 0, 1))


def solution(mesh):
    placed = (
        P(("owner", "dense"), None, None),
        P(("owner", "dense"), None, None),
        P(("owner", "dense"), None, None),
        P(("owner", "dense")),
        P("owner", None),
        P("owner"),
        P(None, "dense"),
        P("dense"),
        P("dense"),
    )
    return jax.shard_map(
        local,
        mesh=mesh,
        in_specs=placed,
        out_specs=(P("owner", None), P("owner"), P(("owner", "dense"), None, None)),
        check_vma=False,
    )
```
